256 devices in a mesh: spin: 2 (over core), orb: 128 (over x, z, y).
Axes of the slice: x: 4, y: 4, z: 8, core: 2. Of those that a mesh axis runs over, the one named last changes fastest.
Arguments:
- orbitals: bfloat16 [2, 512, 64, 4096], P('spin', 'orb'), may hold values from -6 to 6
- exponents: int32 [2, 512], P('spin'), may hold values from -1 to 1
- offsets: int32 [2, 3, 512], P('spin'), may hold values from 0 to 16
- pair_list: int32 [2, 2, 2048], P('spin', None, 'orb'), may hold values from -1 to 511, as said below
Outputs:
- potentials: bfloat16 [2, 512, 64, 4096], P('spin', 'orb')
- energy: float32 [], replicated
The draws below stay inside these ranges and needn't reach their ends.
Inputs may be any that keep to these rules, and one draw needn't show every extreme that they name: `pair_list`: slots 16 g to 16 g + 15 belong to owner group g. In a live slot, i lies in the owner's block of 4 orbitals (orbitals 4 g to 4 g + 3) and j differs from i and lies in that block or in the block just before or just after it, cyclically over the groups. Live slots come first; the other slots hold -1 in both rows. Every owner has two or more live tasks, among them one with j in the block before and one with j in the block after. In each spin some owner has all 16 slots live. A pair may be listed more than once.
All inputs are finite; a program needn't handle non-finite values.
Results may differ from the reference program's by a relative error of at most 0.001.
Values may be sent and summed in bfloat16 or wider, within the bound.
No kernel may reach another device: no remote copies, remote signals or barrier semaphores. Data moves between devices by JAX's collectives and lax.ppermute only.
A program may use at most 128 MiB of HBM per device.

```python
import jax
import jax.numpy as jnp
from jax import lax

B = 64
SHIFT = 16
ORB_DEV = 4
TASK_SLOTS = 16
SPINS = 2
ORBITALS = 512
TASKS = 2048


def draw_pair_list(key, part):
    key = jax.random.fold_in(key, 11)
    group_count = TASKS // TASK_SLOTS
    subkeys = jax.random.split(key, 8)
    task_shape = (SPINS, group_count, TASK_SLOTS)
    extra_tasks = jax.random.randint(subkeys[0], (SPINS, group_count), 0, max(TASK_SLOTS // 4, 1) + 1)
    live_count = 2 + extra_tasks
    busiest = jax.random.randint(subkeys[1], (SPINS,), 0, group_count)
    live_count = jnp.where(jnp.arange(group_count)[None, :] == busiest[:, None], TASK_SLOTS, live_count)
    live_count = jnp.minimum(live_count, TASK_SLOTS)[:, :, None]
    slot_number = jnp.arange(TASK_SLOTS)[None, None, :]
    before_slot = jax.random.randint(subkeys[2], (SPINS, group_count, 1), 0, live_count)
    after_slot = (before_slot + 1 + jax.random.randint(subkeys[3], (SPINS, group_count, 1), 0, live_count - 1)) % live_count
    neighbour_step = jax.random.randint(subkeys[4], task_shape, -1, 2)
    neighbour_step = jnp.where(slot_number == before_slot, -1, jnp.where(slot_number == after_slot, 1, neighbour_step))
    owner_group = jnp.arange(group_count)[None, :, None]
    first_local = jax.random.randint(subkeys[5], task_shape, 0, ORB_DEV)
    other_local = jax.random.randint(subkeys[6], task_shape, 0, ORB_DEV)
    same_local = (first_local + 1 + jax.random.randint(subkeys[7], task_shape, 0, ORB_DEV - 1)) % ORB_DEV
    second_local = jnp.where(neighbour_step == 0, same_local, other_local)
    first_index = owner_group * ORB_DEV + first_local
    second_index = (owner_group + neighbour_step) % group_count * ORB_DEV + second_local
    active = slot_number < live_count
    first_index = jnp.where(active, first_index, -1)
    second_index = jnp.where(active, second_index, -1)
    return jnp.stack([first_index, second_index], axis=1).reshape(SPINS, 2, TASKS).astype(jnp.int32)


def place_ends(array, own_key, low, high):
    longest = array.shape.index(max(array.shape))
    spots = []
    for shift in (0, 1):
        where = [jax.random.randint(jax.random.fold_in(own_key, axis), (), 0, length) for axis, length in enumerate(array.shape)]
        where[longest] = (where[longest] + shift) % array.shape[longest]
        spots.append(tuple(where))
    return array.at[spots[0]].set(low).at[spots[1]].set(high)


def level_of(key, shape, cuts, smallest, high):
    loudness = 1.0
    for axis_at, shards_of in cuts:
        heights = jax.random.uniform(jax.random.fold_in(jax.random.fold_in(key, 6), axis_at), (shards_of,), jnp.float32, smallest / len(cuts), high / len(cuts))
        loudness = loudness * jnp.repeat(jnp.exp(heights), shape[axis_at] // shards_of).reshape((-1,) + (1,) * (len(shape) - 1 - axis_at))
    return loudness


def gaussian(rng, shape, width, limit, cuts=(), held_as=jnp.bfloat16):
    entries = width * jax.random.normal(rng, shape, jnp.float32)
    if cuts:
        entries = entries * level_of(rng, shape, cuts, -0.22, 0.18)
    return jnp.clip(entries, -limit, limit).astype(held_as)


def setup_inputs(seed: int = 0) -> dict:
    keys = jax.random.split(jax.random.key(seed), 5)
    return {
        "orbitals": gaussian(keys[0], (SPINS, ORBITALS, B, B * B), 1.0, 6.0, ((0, 2), (1, 128))),
        "exponents": place_ends(jax.random.randint(keys[1], (SPINS, ORBITALS), -1, 2), jax.random.fold_in(keys[1], 1), -1, 1).astype(jnp.int32),
        "offsets": place_ends(jax.random.randint(keys[2], (SPINS, 3, ORBITALS), 0, SHIFT + 1), jax.random.fold_in(keys[2], 1), 0, SHIFT).astype(jnp.int32),
        "pair_list": draw_pair_list(jax.random.fold_in(keys[4], 71), 0),
    }


FRACTION = 0.25

def sine_matrix(extent):
    wavenumber = jnp.arange(extent, dtype=jnp.float32) + 1.0
    phase_grid = jnp.pi * wavenumber[:, None] * wavenumber[None, :] / (extent + 1)
    return jnp.sqrt(2.0 / (extent + 1)) * jnp.sin(phase_grid)

def eigen_inverse(extent):
    wavenumber = jnp.arange(extent, dtype=jnp.float32) + 1.0
    eigenvalue = 2.0 - 2.0 * jnp.cos(jnp.pi * wavenumber / (extent + 1))
    return 1.0 / (eigenvalue[:, None, None] + eigenvalue[None, :, None] + eigenvalue[None, None, :])

def sine_transform(matrix, values):
    highest = lax.Precision.HIGHEST
    values = jnp.einsum('ka,abc->kbc', matrix, values, precision=highest)
    values = jnp.einsum('kb,abc->akc', matrix, values, precision=highest)
    values = jnp.einsum('kc,abc->abk', matrix, values, precision=highest)
    return values

def pair_terms(matrix, inverse, first_box, second_box, displacement):
    extent = first_box.shape[0]
    padded = jnp.pad(second_box, SHIFT)
    begin = (displacement + SHIFT).astype(jnp.int32)
    second_here = lax.dynamic_slice(padded, (begin[0], begin[1], begin[2]), (extent, extent, extent))
    density = first_box * second_here
    potential = sine_transform(matrix, inverse * sine_transform(matrix, density))
    pair_energy = jnp.sum(density * potential)
    to_first = potential * second_here
    back = (SHIFT - displacement).astype(jnp.int32)
    moved_term = lax.dynamic_slice(jnp.pad(potential * first_box, SHIFT), (back[0], back[1], back[2]), (extent, extent, extent))
    return (to_first, moved_term, pair_energy)

def reference(orbitals, exponents, offsets, pair_list):
    extent = orbitals.shape[2]
    matrix = sine_matrix(extent)
    inverse = eigen_inverse(extent)
    results = []
    energy_sum = jnp.zeros((), jnp.float32)
    for spin_index in range(orbitals.shape[0]):
        spin_boxes = orbitals[spin_index]
        orbital_scale = jnp.exp2(exponents[spin_index].astype(jnp.float32))
        box_anchor = offsets[spin_index]
        task_table = pair_list[spin_index]

        def advance(loop_state, slot_number):
            totals, running = loop_state
            first_index = task_table[0, slot_number]
            second_index = task_table[1, slot_number]
            active = first_index >= 0
            first_index = jnp.maximum(first_index, 0)
            second_index = jnp.maximum(second_index, 0)
            first_box = spin_boxes[first_index].astype(jnp.float32).reshape(extent, extent, extent) * orbital_scale[first_index]
            second_box = spin_boxes[second_index].astype(jnp.float32).reshape(extent, extent, extent) * orbital_scale[second_index]
            displacement = box_anchor[:, first_index] - box_anchor[:, second_index]
            to_first, moved_term, pair_energy = pair_terms(matrix, inverse, first_box, second_box, displacement)
            weight = jnp.where(active, -FRACTION, 0.0)
            totals = totals.at[first_index].add(weight * to_first.reshape(extent, extent * extent))
            totals = totals.at[second_index].add(weight * moved_term.reshape(extent, extent * extent))
            running = running + jnp.where(active, pair_energy, 0.0)
            return ((totals, running), None)
        initial = (jnp.zeros(spin_boxes.shape, jnp.float32), jnp.zeros((), jnp.float32))
        (totals, running), _ = lax.scan(advance, initial, jnp.arange(task_table.shape[1]))
        results.append(totals.astype(jnp.bfloat16))
        energy_sum = energy_sum + running
    return (jnp.stack(results), -FRACTION / extent ** 3 * energy_sum)
```

```python
import functools

import jax
import jax.numpy as jnp
import numpy as np
from jax import lax
from jax.experimental import pallas as pl
from jax.experimental.pallas import tpu as pltpu
from jax.sharding import PartitionSpec as P

FRACTION = 0.25
N = 64
H = N // 2
L = 2 * N
SHIFT = 16
PAD = SHIFT // 2 + 1
ROWS = H * N
BLOCKS = 8
CHUNKS = (2, 2)


def split_np(matrix):
    high = matrix.astype(jnp.bfloat16).astype(np.float64)
    low = (matrix - high).astype(jnp.bfloat16).astype(np.float64)
    return high, low


def tables():
    k = np.arange(N, dtype=np.float64) + 1.0
    sine = np.sqrt(2.0 / (N + 1)) * np.sin(np.pi * k[:, None] * k[None, :] / (N + 1))
    high, low = split_np(sine)
    two = lambda m: np.kron(np.eye(2), m)
    lane = np.block([[two(high), two(low)], [two(high), two(low)]])
    sublane = lane.T
    lam = 2.0 - 2.0 * np.cos(np.pi * k / (N + 1))
    diagonal = 2.0 + lam[:, None] + lam[None, :]
    coef = np.zeros((H, N, N))
    coef[0] = 1.0 / diagonal
    for s in range(1, H):
        coef[s] = 1.0 / (diagonal - coef[s - 1])
    middle = 1.0 / (1.0 - coef[-1] ** 2)
    coef = np.concatenate([coef, middle[None]], axis=0)
    coef = np.concatenate([coef, coef], axis=2).reshape((H + 1) * N, L)
    return (
        lane.astype(jnp.bfloat16),
        sublane.astype(jnp.bfloat16),
        coef.astype(np.float32),
    )


def split(x):
    high = x.astype(jnp.bfloat16)
    low = (x - high.astype(jnp.float32)).astype(jnp.bfloat16)
    return high, low


def lane_transform(x, lane_ref):
    high, low = split(x)
    out = jnp.dot(
        jnp.concatenate([high, low], axis=1), lane_ref[...], preferred_element_type=jnp.float32
    )
    return out[:, :L] + out[:, L:]


def sublane_transform(x, sublane_ref):
    high, low = split(x)
    half = 2 * N
    data = jnp.concatenate(
        [
            jnp.concatenate([high[:half], high[half:]], axis=1),
            jnp.concatenate([low[:half], low[half:]], axis=1),
        ],
        axis=0,
    )
    out = jnp.dot(sublane_ref[...], data, preferred_element_type=jnp.float32)
    out = out[:half] + out[half:]
    return jnp.concatenate([out[:, :L], out[:, L:]], axis=0)


def low_lanes(shape):
    return lax.broadcasted_iota(jnp.int32, shape, 1) < N


def tile_rows(t):
    return pl.ds(pl.multiple_of(t * N, N), N)


def tile_lanes(t):
    return pl.ds(pl.multiple_of(t * L, L), L)


def clear_pads(pad_ref):
    ends = SHIFT + PAD * N
    pad_ref[pl.ds(0, ends), :] = jnp.zeros((ends, L), jnp.float32)
    pad_ref[pl.ds(ends + ROWS, ends), :] = jnp.zeros((ends, L), jnp.float32)


def pad_rows(t):
    return pl.ds(pl.multiple_of(SHIFT + (PAD + t) * N, 8), N)


def shifted_reader(pad_ref, displacement, factor):
    da, db, dc = displacement
    flat = db * N + dc
    turn = lax.rem(flat + 16 * L, L)
    jump = lax.div(flat + 16 * L, L) - 16
    lane = lax.broadcasted_iota(jnp.int32, (N, L), 1)
    cell = lane % N + dc
    plane = lax.broadcasted_iota(jnp.int32, (N, L), 0) + da
    inside = (cell >= 0) & (cell < N) & (plane >= 0) & (plane < N)
    weight = jnp.where(inside, factor, 0.0)
    from_next = lane < turn
    back_turn = lax.rem(L - turn, L)

    def read(t):
        start = SHIFT + (PAD + t + jump) * N + da
        here = pad_ref[pl.ds(start, N), :]
        following = pad_ref[pl.ds(start + N, N), :]
        both = jnp.where(from_next, following, here)
        return pltpu.roll(both, back_turn, 1) * weight

    return read


def solve_task(refs, i_box, j_box, displacement, factor, wants_first, wants_second, i_acc, j_acc):
    (lane_ref, sublane_ref, coef_ref, pad_ref, acc_ref, energy_ref, rj_ref, z_ref) = refs
    low = low_lanes((N, L))

    def spread(t, carry):
        pad_ref[pad_rows(t), :] = j_box[:, tile_lanes(t)].astype(jnp.float32)
        return carry

    lax.fori_loop(0, H, spread, 0, unroll=4)
    read = shifted_reader(pad_ref, displacement, factor)

    def rows_of(step):
        t = 2 * step
        return (t, t + 1, H - 1 - t, H - 2 - t)

    def forward(step, g):
        for block in range(BLOCKS):
            s = step * BLOCKS + block
            rows = rows_of(s)
            rho = []
            for t in rows:
                seen = read(t)
                rj_ref[tile_rows(t), :] = seen
                rho.append(i_box[:, tile_lanes(t)].astype(jnp.float32) * seen)
            x = lane_transform(jnp.concatenate(rho, axis=0), lane_ref)
            x = sublane_transform(x, sublane_ref)
            x = [x[k * N : (k + 1) * N] for k in range(4)]
            for k in range(2):
                near, far = x[k], x[2 + k]
                t = rows[k]
                g = coef_ref[tile_rows(2 * t), :] * (jnp.where(low, near, far) + g)
                z_ref[tile_rows(2 * t), :] = g
                odd = pltpu.roll(jnp.where(low, far, near), N, 1)
                g = coef_ref[tile_rows(2 * t + 1), :] * (odd + g)
                z_ref[tile_rows(2 * t + 1), :] = g
        return g

    steps = H // 4 // BLOCKS
    g = lax.fori_loop(0, steps, forward, jnp.zeros((N, L), jnp.float32))
    z = (g + coef_ref[tile_rows(H - 1), :] * pltpu.roll(g, N, 1)) * coef_ref[tile_rows(H), :]

    def inverse(step, carry):
        z, energy = carry
        for block in range(BLOCKS):
            s = H // 4 - 1 - (step * BLOCKS + block)
            rows = rows_of(s)
            x = [None] * 4
            for k in (1, 0):
                t = rows[k]
                odd = z_ref[tile_rows(2 * t + 1), :] + coef_ref[tile_rows(2 * t + 1), :] * z
                z = z_ref[tile_rows(2 * t), :] + coef_ref[tile_rows(2 * t), :] * odd
                turned = pltpu.roll(odd, N, 1)
                x[k] = jnp.where(low, z, turned)
                x[2 + k] = jnp.where(low, turned, z)
            v = sublane_transform(jnp.concatenate(x, axis=0), sublane_ref)
            v = lane_transform(v, lane_ref)
            for k, t in enumerate(rows):
                part = v[k * N : (k + 1) * N]
                phi = i_box[:, tile_lanes(t)].astype(jnp.float32)
                if wants_first:
                    to_first = part * rj_ref[tile_rows(t), :]
                    acc_ref[i_acc, :, tile_lanes(t)] += to_first
                    energy = energy + (to_first * phi).reshape(N // 8, 8, L).sum(axis=0)
                if wants_second:
                    pad_ref[pad_rows(t), :] = part * phi
        return z, energy

    start = (jnp.zeros((N, L), jnp.float32), jnp.zeros((8, L), jnp.float32))
    z_ref[tile_rows(H - 1), :] = z
    _, energy = lax.fori_loop(0, steps, inverse, start)
    if wants_first:
        energy_ref[...] += energy
    if wants_second:
        read_back = shifted_reader(pad_ref, [-d for d in displacement], factor)

        def add_back(t, carry):
            acc_ref[j_acc, :, tile_lanes(t)] += read_back(t)
            return carry

        lax.fori_loop(0, H, add_back, 0, unroll=4)


def stage_kernel(places, last, peers, *refs):
    first = not places
    me_ref, offsets_ref, exponents_ref = refs[:3]
    tables = refs[3 : 4 if first else 6]
    refs = refs[3 + len(tables) :]
    own_ref, consts, refs = refs[0], refs[1:4], refs[4:]
    if not first:
        halo_in, (acc_in, energy_in), refs = refs[:2], refs[2:4], refs[4:]
    out_ref, energy_out, pad_ref, rj_ref, z_ref, energy_ref = refs[:6]
    refs = refs[6:]
    acc_ref = out_ref
    if last:
        acc_ref, refs = refs[0], refs[1:]
    block = own_ref.shape[0]
    groups = exponents_ref.shape[0] // block
    slots = tables[0].shape[1]
    me = me_ref[0]
    group_before = lax.rem(me + groups - 1, groups)

    if first:
        clear_pads(pad_ref)
        acc_ref[...] = jnp.zeros_like(acc_ref)
        energy_ref[...] = jnp.zeros_like(energy_ref)
    else:
        halo_ref, sems = refs
        copies = [
            pltpu.make_async_copy(halo_in[side], halo_ref.at[side], sems.at[side]) for side in (0, 1)
        ]
        acc_copy = pltpu.make_async_copy(acc_in, acc_ref, sems.at[2])
        for copy in copies:
            copy.start()
        acc_copy.start()
        clear_pads(pad_ref)
        energy_ref[...] = energy_in[...]
        for copy in copies:
            copy.wait()
        acc_copy.wait()
    refs = tuple(consts) + (pad_ref, acc_ref, energy_ref, rj_ref, z_ref)

    def power(exponent):
        return jnp.exp2(jnp.full((N, L), exponent, jnp.int32).astype(jnp.float32))

    def run(i, j, i_box, j_box, wants_first, wants_second):
        solve_task(
            refs,
            i_box,
            j_box,
            [offsets_ref[k, i] - offsets_ref[k, j] for k in range(3)],
            power(exponents_ref[i] + exponents_ref[j]),
            wants_first,
            wants_second,
            lax.rem(i, block),
            lax.rem(j, block),
        )

    def place_of(index):
        local = lax.rem(index, block) - places[0]
        return jnp.where((local >= 0) & (local < len(places)), local, -1)

    def visit_own(slot, carry):
        i = tables[-2 if not first else 0][0, slot]
        j = tables[-2 if not first else 0][1, slot]
        j_group = lax.div(j, block)
        if first:

            @pl.when((i >= 0) & (j_group == me))
            def _():
                run(i, j, own_ref.at[lax.rem(i, block)], own_ref.at[lax.rem(j, block)], True, True)

        else:
            place = place_of(j)

            @pl.when((i >= 0) & (j_group != me) & (place >= 0))
            def _():
                side = jnp.where(j_group == group_before, 0, 1)
                run(i, j, own_ref.at[lax.rem(i, block)], halo_ref.at[side, place], True, False)

        return carry

    lax.fori_loop(0, slots, visit_own, 0)

    def visit_others(number, carry):
        side = lax.div(number, slots)
        slot = lax.rem(number, slots)
        i = jnp.where(side == 0, tables[0][0, slot], tables[2][0, slot])
        j = jnp.where(side == 0, tables[0][1, slot], tables[2][1, slot])
        place = place_of(i)

        @pl.when((i >= 0) & (lax.div(j, block) == me) & (place >= 0))
        def _():
            run(i, j, halo_ref.at[side, place], own_ref.at[lax.rem(j, block)], False, True)

        return carry

    if not first:
        lax.fori_loop(0, 2 * slots, visit_others, 0)

    if last:
        energy_out[...] = jnp.full((peers, L), jnp.sum(energy_ref[...]), jnp.float32)
        for k in range(block):
            scale = -FRACTION * power(-exponents_ref[me * block + k])

            def write(t, carry):
                out_ref[k, :, tile_lanes(t)] = (acc_ref[k, :, tile_lanes(t)] * scale).astype(
                    jnp.bfloat16
                )
                return carry

            lax.fori_loop(0, H, write, 0, unroll=4)
    else:
        energy_out[...] = energy_ref[...]


def stage(places, last, peers, scalars, tables, own, halo, consts, state):
    acc_shape = jax.ShapeDtypeStruct(own.shape, jnp.float32)
    out_shape = jax.ShapeDtypeStruct(own.shape, own.dtype) if last else acc_shape
    energy_shape = jax.ShapeDtypeStruct((peers if last else 8, L), jnp.float32)
    smem = pl.BlockSpec(memory_space=pltpu.SMEM)
    vmem = pl.BlockSpec(memory_space=pltpu.VMEM)
    hbm = pl.BlockSpec(memory_space=pl.ANY)
    operands = list(scalars) + list(tables) + [own] + list(consts)
    specs = [smem] * (len(scalars) + len(tables)) + [vmem] * (1 + len(consts))
    if places:
        operands += list(halo) + list(state)
        specs += [hbm] * 3 + [vmem]
    scratch = [
        pltpu.VMEM(((H + 2 * PAD) * N + 2 * SHIFT, L), jnp.float32),
        pltpu.VMEM((ROWS, L), jnp.float32),
        pltpu.VMEM((ROWS, L), jnp.float32),
        pltpu.VMEM((8, L), jnp.float32),
    ]
    if last:
        scratch.append(pltpu.VMEM(acc_shape.shape, jnp.float32))
    if places:
        scratch.append(pltpu.VMEM((2, len(places)) + own.shape[1:], own.dtype))
        scratch.append(pltpu.SemaphoreType.DMA((3,)))
    return pl.pallas_call(
        functools.partial(stage_kernel, places, last, peers),
        out_shape=(out_shape, energy_shape),
        in_specs=specs,
        out_specs=(vmem, vmem),
        scratch_shapes=scratch,
        compiler_params=pltpu.CompilerParams(vmem_limit_bytes=56 * 2**20),
        cost_estimate=pl.CostEstimate(flops=2 * 10**10, bytes_accessed=10**7, transcendentals=0),
    )(*operands)


def on_device(orbitals, exponents, offsets, pair_list):
    own = orbitals[0]
    block = own.shape[0]
    groups = lax.axis_size("orb")
    peers = groups * lax.axis_size("spin")
    me = lax.axis_index("orb").astype(jnp.int32).reshape(1)
    up = [(k, (k + 1) % groups) for k in range(groups)]
    down = [(k, j) for j, k in up]
    table = pair_list[0]
    scalars = (me, offsets[0], exponents[0])
    consts = tuple(jnp.asarray(c) for c in tables())
    chunks = CHUNKS if sum(CHUNKS) == block else (block,)
    around = (lax.ppermute(table, "orb", up), table, lax.ppermute(table, "orb", down))
    around, own_sent = lax.optimization_barrier((around, own))
    halo, places = [], []
    for size in chunks:
        start = sum(len(p) for p in places)
        places.append(tuple(range(start, start + size)))
        part = own_sent[start : start + size]
        halo.append((lax.ppermute(part, "orb", up), lax.ppermute(part, "orb", down)))
    state = stage((), False, peers, scalars, (table,), own, (), consts, None)
    for n, place in enumerate(places):
        last = n == len(places) - 1
        state = stage(place, last, peers, scalars, around, own, halo[n], consts, state)
    potentials, energy = state
    energies = lax.all_to_all(energy, ("spin", "orb"), 0, 0)
    total = jnp.sum(energies[:, 0])
    return (potentials[None], -FRACTION / N**3 * total)


def solution(mesh):
    in_specs = (
        P("spin", "orb", None, None),
        P("spin", None),
        P("spin", None, None),
        P("spin", None, "orb"),
    )
    out_specs = (P("spin", "orb", None, None), P())
    return jax.shard_map(
        on_device, mesh=mesh, in_specs=in_specs, out_specs=out_specs, check_vma=False
    )
```

```python
import functools

import jax
import jax.numpy as jnp
import numpy as np
from jax import lax
from jax.experimental import pallas as pl
from jax.experimental.pallas import tpu as pltpu
from jax.sharding import PartitionSpec as P

FRACTION = 0.25
N = 64
H = N // 2
L = 2 * N
SHIFT = 16
PAD = SHIFT // 2 + 1
ROWS = H * N
EARLY = 2
LIST = 16


def split_np(matrix):
    high = matrix.astype(jnp.bfloat16).astype(np.float64)
    low = (matrix - high).astype(jnp.bfloat16).astype(np.float64)
    return high, low


def tables():
    k = np.arange(N, dtype=np.float64) + 1.0
    sine = np.sqrt(2.0 / (N + 1)) * np.sin(np.pi * k[:, None] * k[None, :] / (N + 1))
    high, low = split_np(sine)
    two = lambda m: np.kron(np.eye(2), m)
    lane = np.block([[two(high), two(low)], [two(high), two(low)]])
    sublane = lane.T
    lam = 2.0 - 2.0 * np.cos(np.pi * k / (N + 1))
    diagonal = 2.0 + lam[:, None] + lam[None, :]
    coef = np.zeros((H, N, N))
    coef[0] = 1.0 / diagonal
    for s in range(1, H):
        coef[s] = 1.0 / (diagonal - coef[s - 1])
    middle = 1.0 / (1.0 - coef[-1] ** 2)
    coef = np.concatenate([coef, middle[None]], axis=0)
    coef = np.concatenate([coef, coef], axis=2).reshape((H + 1) * N, L)
    return (
        lane.astype(jnp.bfloat16),
        sublane.astype(jnp.bfloat16),
        coef.astype(np.float32),
    )


def split(x):
    high = x.astype(jnp.bfloat16)
    low = (x - high.astype(jnp.float32)).astype(jnp.bfloat16)
    return high, low


def lane_transform(x, lane_ref):
    high, low = split(x)
    out = jnp.dot(
        jnp.concatenate([high, low], axis=1), lane_ref[...], preferred_element_type=jnp.float32
    )
    return out[:, :L] + out[:, L:]


def sublane_transform(x, sublane_ref):
    high, low = split(x)
    half = 2 * N
    data = jnp.concatenate(
        [
            jnp.concatenate([high[:half], high[half:]], axis=1),
            jnp.concatenate([low[:half], low[half:]], axis=1),
        ],
        axis=0,
    )
    out = jnp.dot(sublane_ref[...], data, preferred_element_type=jnp.float32)
    out = out[:half] + out[half:]
    return jnp.concatenate([out[:, :L], out[:, L:]], axis=0)


def low_lanes(shape):
    return lax.broadcasted_iota(jnp.int32, shape, 1) < N


def tile_rows(t):
    return pl.ds(t * N, N) if isinstance(t, int) else pl.ds(pl.multiple_of(t * N, N), N)


def tile_lanes(t):
    return pl.ds(t * L, L) if isinstance(t, int) else pl.ds(pl.multiple_of(t * L, L), L)


def clear_pads(pad_ref):
    ends = SHIFT + PAD * N
    pad_ref[pl.ds(0, ends), :] = jnp.zeros((ends, L), jnp.float32)
    pad_ref[pl.ds(ends + ROWS, ends), :] = jnp.zeros((ends, L), jnp.float32)


def pad_rows(t):
    start = SHIFT + (PAD + t) * N
    return pl.ds(start if isinstance(t, int) else pl.multiple_of(start, 8), N)


def shifted_reader(pad_ref, displacement, factor):
    da, db, dc = displacement
    flat = db * N + dc
    turn = lax.rem(flat + 16 * L, L)
    jump = lax.div(flat + 16 * L, L) - 16
    lane = lax.broadcasted_iota(jnp.int32, (N, L), 1)
    cell = lane % N + dc
    plane = lax.broadcasted_iota(jnp.int32, (N, L), 0) + da
    inside = (cell >= 0) & (cell < N) & (plane >= 0) & (plane < N)
    weight = jnp.where(inside, factor, 0.0)
    from_next = lane < turn
    back_turn = lax.rem(L - turn, L)

    def read(t):
        start = SHIFT + (PAD + t + jump) * N + da
        here = pad_ref[pl.ds(start, N), :]
        following = pad_ref[pl.ds(start + N, N), :]
        both = jnp.where(from_next, following, here)
        return pltpu.roll(both, back_turn, 1) * weight

    return read


def solve_task(
    refs, i_box, j_box, displacement, factor, times, share, wants_first, wants_second, i_acc, j_acc
):
    (lane_ref, sublane_ref, coef_ref, pad_ref, acc_ref, energy_ref, rj_ref, z_ref) = refs
    low = low_lanes((N, L))

    solves = wants_first or wants_second
    for t in range(H):
        pad_ref[pad_rows(t), :] = j_box[:, tile_lanes(t)].astype(jnp.float32)
    read = shifted_reader(pad_ref, displacement, factor)

    def rows_of(step):
        t = 2 * step
        return (t, t + 1, H - 1 - t, H - 2 - t)

    g = jnp.zeros((N, L), jnp.float32)
    energy = jnp.zeros((8, L), jnp.float32)
    for step in range(H // 4):
        rows = rows_of(step)
        rho = []
        for t in rows:
            seen = read(t)
            phi = i_box[:, tile_lanes(t)].astype(jnp.float32)
            if solves:
                rj_ref[tile_rows(t), :] = seen
                phi = phi * times
            rho.append(phi * seen)
        x = lane_transform(jnp.concatenate(rho, axis=0), lane_ref)
        x = sublane_transform(x, sublane_ref)
        x = [x[k * N : (k + 1) * N] for k in range(4)]
        for k in range(2):
            near, far = x[k], x[2 + k]
            odd = pltpu.roll(jnp.where(low, far, near), N, 1)
            for cell, right in ((2 * rows[k], jnp.where(low, near, far)), (2 * rows[k] + 1, odd)):
                right = right + g
                g = coef_ref[tile_rows(cell), :] * right
                value = g
                if cell == H - 1:
                    value = g + coef_ref[tile_rows(cell), :] * pltpu.roll(g, N, 1)
                    value = value * coef_ref[tile_rows(H), :]
                if solves:
                    z_ref[tile_rows(cell), :] = value
                else:
                    energy = energy + (right * value).reshape(N // 8, 8, L).sum(axis=0)
    if not solves:
        energy_ref[...] += energy * (share * times)
        return

    z = None
    for step in reversed(range(H // 4)):
        rows = rows_of(step)
        x = [None] * 4
        for k in (1, 0):
            t = rows[k]
            odd = z_ref[tile_rows(2 * t + 1), :]
            if z is not None:
                odd = odd + coef_ref[tile_rows(2 * t + 1), :] * z
            z = z_ref[tile_rows(2 * t), :] + coef_ref[tile_rows(2 * t), :] * odd
            turned = pltpu.roll(odd, N, 1)
            x[k] = jnp.where(low, z, turned)
            x[2 + k] = jnp.where(low, turned, z)
        v = sublane_transform(jnp.concatenate(x, axis=0), sublane_ref)
        v = lane_transform(v, lane_ref)
        for k, t in enumerate(rows):
            part = v[k * N : (k + 1) * N]
            phi = i_box[:, tile_lanes(t)].astype(jnp.float32)
            to_first = part * rj_ref[tile_rows(t), :]
            energy = energy + (to_first * phi).reshape(N // 8, 8, L).sum(axis=0)
            if wants_first:
                acc_ref[i_acc, :, tile_lanes(t)] += to_first
            if wants_second:
                pad_ref[pad_rows(t), :] = part * phi
    energy_ref[...] += energy * share
    if wants_second:
        read_back = shifted_reader(pad_ref, [-d for d in displacement], factor)

        for t in range(H):
            acc_ref[j_acc, :, tile_lanes(t)] += read_back(t)


SMEM = pl.BlockSpec(memory_space=pltpu.SMEM)
VMEM = pl.BlockSpec(memory_space=pltpu.VMEM)
HBM = pl.BlockSpec(memory_space=pltpu.HBM)
ANY = pl.BlockSpec(memory_space=pl.ANY)


def stage_kernel(kind, *refs):
    me_ref, offsets_ref, exponents_ref, tables_ref, own_in = refs[:5]
    consts_in, refs = refs[5:8], refs[8:]
    halo_in = earlier_in = energy_in = out_ref = energy_out = None
    if kind != "own":
        halo_in, refs = refs[:2], refs[2:]
    if kind in ("near", "rest"):
        energy_in, refs = refs[0], refs[1:]
    if kind == "far":
        earlier_in, refs = refs[:2], refs[2:]
    if kind != "rest":
        out_ref, refs = refs[0], refs[1:]
    if kind != "far":
        energy_out, refs = refs[0], refs[1:]
    if kind == "own":
        sent, refs = refs[0], refs[1:]
    energy_ref, pad_ref, rj_ref, z_ref, sems, own_ref = refs[:6]
    consts, refs = refs[6:9], refs[9:]
    copies = [(own_in, own_ref)] + list(zip(consts_in, consts))
    if kind != "own":
        halo_ref, refs = refs[0], refs[1:]
        for side in (0, 1):
            for k in range(EARLY):
                box = halo_in[side].at[pl.ds(k * N, N), :]
                copies.append((box, halo_ref.at[side, k]))
    copies = [pltpu.make_async_copy(x, y, sems.at[k]) for k, (x, y) in enumerate(copies)]
    for copy in copies:
        copy.start()
    acc_ref = None
    if kind != "rest":
        acc_ref, refs = refs[0], refs[1:]
    if kind == "far":
        earlier_ref = refs[0]
        earlier = [
            pltpu.make_async_copy(earlier_in[n], earlier_ref.at[n], sems.at[8 + n]) for n in (0, 1)
        ]
        for copy in earlier:
            copy.start()

    block = own_ref.shape[0]
    groups = exponents_ref.shape[0] // block
    slots = tables_ref.shape[1]
    me = me_ref[0]

    clear_pads(pad_ref)
    energy_ref[...] = jnp.zeros_like(energy_ref) if energy_in is None else energy_in[...]
    if acc_ref is not None:
        acc_ref[...] = jnp.zeros_like(acc_ref)
    for copy in copies:
        copy.wait()
    if kind == "own":
        others = [
            pltpu.make_async_copy(own_ref.at[EARLY + k], sent.at[pl.ds(k * N, N), :], sems.at[4 + k])
            for k in range(block - EARLY)
        ]
        for copy in others:
            copy.start()
    refs = tuple(consts) + (pad_ref, acc_ref, energy_ref, rj_ref, z_ref)

    def power(exponent):
        return jnp.exp2(jnp.full((N, L), exponent, jnp.int32).astype(jnp.float32))

    def run(owner, slot, i_box, j_box, share, wants_first, wants_second):
        row = 0 if kind == "own" else 2 * owner
        local, code = tables_ref[row, slot], tables_ref[row + 1, slot]

        def look(k, found):
            same = ((tables_ref[row, k] == local) & (tables_ref[row + 1, k] == code)).astype(jnp.int32)
            return found[0] + same, found[1] + jnp.where(k < slot, same, 0)

        times, sooner = lax.fori_loop(
            0, slots, look, (jnp.int32(0), jnp.int32(0)), unroll=True
        )

        @pl.when(sooner == 0)
        def _():
            group = me + owner - 1 + groups
            i = lax.rem(group, groups) * block + local
            j = lax.rem((group - 1) * block + code, groups * block)
            solve_task(
                refs,
                i_box,
                j_box,
                [offsets_ref[k, i] - offsets_ref[k, j] for k in range(3)],
                power(exponents_ref[i] + exponents_ref[j]),
                times.astype(jnp.float32),
                jnp.asarray(share).astype(jnp.float32),
                wants_first,
                wants_second,
                local,
                code & (block - 1),
            )

    def in_chunk(local):
        if kind == "near":
            return local < EARLY, jnp.minimum(local, EARLY - 1)
        return local >= EARLY, jnp.maximum(local - EARLY, 0)

    def live_of(row):
        return lax.fori_loop(
            0, slots, lambda k, n: n + (tables_ref[row, k] >= 0).astype(jnp.int32), jnp.int32(0), unroll=True
        )

    def visit_own(slot, carry):
        row = 0 if kind == "own" else 2
        local, code = tables_ref[row, slot], tables_ref[row + 1, slot]
        other, group = code & (block - 1), lax.div(code, block)
        if kind == "own":

            @pl.when(group == 1)
            def _():
                run(1, slot, own_ref.at[local], own_ref.at[other], 1, True, True)

            return carry
        chosen, at = in_chunk(other)
        chosen = chosen & (group != 1)
        if kind == "rest":
            chosen = chosen & (local >= EARLY)
        side = jnp.where(group == 0, 0, 1)
        wants = kind != "rest"

        @pl.when(chosen)
        def _():
            share = 0 if kind == "far" else 1
            run(1, slot, own_ref.at[local], halo_ref.at[side, at], share, wants, False)

        return carry

    lax.fori_loop(0, live_of(0 if kind == "own" else 2), visit_own, 0)

    if kind in ("near", "far"):
        live_before = live_of(0)

        def visit_others(k, carry):
            side = (k >= live_before).astype(jnp.int32)
            slot = k - side * live_before
            local, code = tables_ref[4 * side, slot], tables_ref[4 * side + 1, slot]
            other = code & (block - 1)
            chosen, at = in_chunk(local)
            mine = lax.div(code, block) == 2 - 2 * side

            @pl.when(chosen & mine)
            def _():
                share = other >= EARLY if kind == "near" else 0
                run(2 * side, slot, halo_ref.at[side, at], own_ref.at[other], share, False, True)

            return carry

        lax.fori_loop(0, live_before + live_of(4), visit_others, 0)

    if kind == "rest":
        energy_out[...] = jnp.full(energy_out.shape, jnp.sum(energy_ref[...]), jnp.float32)
    elif kind != "far":
        energy_out[...] = energy_ref[...]
    if kind in ("own", "near"):
        copy = pltpu.make_async_copy(acc_ref, out_ref, sems.at[0])
        copy.start()
        copy.wait()
        if kind == "own":
            for copy in others:
                copy.wait()
    if kind == "far":
        for copy in earlier:
            copy.wait()
        for k in range(block):
            scale = -FRACTION * power(-exponents_ref[me * block + k])

            def write(t, carry):
                lanes = tile_lanes(t)
                total = earlier_ref[0, k, :, lanes] + earlier_ref[1, k, :, lanes] + acc_ref[k, :, lanes]
                out_ref[k, :, lanes] = (total * scale).astype(jnp.bfloat16)
                return carry

            lax.fori_loop(0, H, write, 0, unroll=4)


def stage(kind, peers, scalars, own, consts, halo=(), earlier=(), energy=None):
    totals = jax.ShapeDtypeStruct(own.shape, jnp.float32)
    operands = list(scalars) + [own] + list(consts) + list(halo) + list(earlier)
    specs = [SMEM] * len(scalars) + [ANY] + [HBM] * 3 + [ANY] * len(halo) + [HBM] * len(earlier)
    if energy is not None:
        operands.append(energy)
        specs.append(VMEM)
    out_shapes, out_specs = [], []
    if kind != "rest":
        out_shapes.append(jax.ShapeDtypeStruct(own.shape, own.dtype) if kind == "far" else totals)
        out_specs.append(VMEM if kind == "far" else HBM)
    if kind != "far":
        out_shapes.append(jax.ShapeDtypeStruct((peers if kind == "rest" else 8, L), jnp.float32))
        out_specs.append(VMEM)
    if kind == "own":
        others = (own.shape[0] - EARLY) * own.shape[1]
        out_shapes.append(jax.ShapeDtypeStruct((others, own.shape[2]), own.dtype))
        out_specs.append(HBM)
    scratch = [
        pltpu.VMEM((8, L), jnp.float32),
        pltpu.VMEM(((H + 2 * PAD) * N + 2 * SHIFT, L), jnp.float32),
        pltpu.VMEM((ROWS, L), jnp.float32),
        pltpu.VMEM((ROWS, L), jnp.float32),
        pltpu.SemaphoreType.DMA((10,)),
        pltpu.VMEM(own.shape, own.dtype),
    ] + [pltpu.VMEM(c.shape, c.dtype) for c in consts]
    if halo:
        scratch.append(pltpu.VMEM((2, EARLY) + own.shape[1:], own.dtype))
    if kind != "rest":
        scratch.append(pltpu.VMEM(own.shape, jnp.float32))
    if kind == "far":
        scratch.append(pltpu.VMEM((2,) + own.shape, jnp.float32))
    return pl.pallas_call(
        functools.partial(stage_kernel, kind),
        out_shape=out_shapes,
        in_specs=specs,
        out_specs=out_specs,
        scratch_shapes=scratch,
        compiler_params=pltpu.CompilerParams(vmem_limit_bytes=56 * 2**20),
        cost_estimate=pl.CostEstimate(flops=2 * 10**10, bytes_accessed=10**7, transcendentals=0),
    )(*operands)


def on_device(orbitals, exponents, offsets, pair_list):
    own = orbitals[0]
    block, _, width = own.shape
    groups = lax.axis_size("orb")
    peers = groups * lax.axis_size("spin")
    me = lax.axis_index("orb").astype(jnp.int32).reshape(1)
    up = [(k, (k + 1) % groups) for k in range(groups)]
    down = [(k, j) for j, k in up]
    consts = tuple(jnp.asarray(c) for c in tables())

    def exchange(array):
        return lax.ppermute(array, "orb", up), lax.ppermute(array, "orb", down)

    first, second = pair_list[0]
    live = first >= 0
    base = (me - 1) * block
    code = jnp.where(second < base, second + groups * block, second) - base
    code = jnp.where(code >= groups * block, code - groups * block, code)
    table = jnp.stack([jnp.where(live, first - me * block, -1), jnp.where(live, code, -1)])
    listing = jnp.pad(table.astype(own.dtype), ((0, LIST - 2), (0, width - table.shape[1])))
    near = exchange(jnp.concatenate([own[:EARLY].reshape(EARLY * N, width), listing], axis=0))
    rows = slice(EARLY * N, EARLY * N + 2)
    lists = [x[rows, : table.shape[1]].astype(jnp.int32) for x in near]
    around = jnp.concatenate([lists[0], table, lists[1]], axis=0)

    scalars = (me, offsets[0], exponents[0])
    acc, energy, others = stage("own", peers, scalars + (table,), own, consts)
    far = exchange(others)
    scalars += (around,)
    more, energy = stage("near", peers, scalars, own, consts, near, energy=energy)
    (rows,) = stage("rest", peers, scalars, own, consts, far, energy=energy)
    rows = lax.all_to_all(rows, ("spin", "orb"), 0, 0)
    (potentials,) = stage("far", peers, scalars, own, consts, far, (acc, more))
    return (potentials[None], -FRACTION / N**3 * jnp.sum(rows[:, 0]))


def solution(mesh):
    in_specs = (
        P("spin", "orb", None, None),
        P("spin", None),
        P("spin", None, None),
        P("spin", None, "orb"),
    )
    out_specs = (P("spin", "orb", None, None), P())
    return jax.shard_map(
        on_device, mesh=mesh, in_specs=in_specs, out_specs=out_specs, check_vma=False
    )
```

```python
import functools

import jax
import jax.numpy as jnp
import numpy as np
from jax import lax
from jax.experimental import pallas as pl
from jax.experimental.pallas import tpu as pltpu
from jax.sharding import PartitionSpec as P

FRACTION = 0.25
N = 64
H = N // 2
L = 2 * N
SHIFT = 16
PAD = SHIFT // 2 + 1
ROWS = H * N
EARLY = 2
LIST = 16


def split_np(matrix):
    high = matrix.astype(jnp.bfloat16).astype(np.float64)
    low = (matrix - high).astype(jnp.bfloat16).astype(np.float64)
    return high, low


def tables():
    k = np.arange(N, dtype=np.float64) + 1.0
    sine = np.sqrt(2.0 / (N + 1)) * np.sin(np.pi * k[:, None] * k[None, :] / (N + 1))
    high, low = split_np(sine)
    two = lambda m: np.kron(np.eye(2), m)
    lane = np.block([[two(high), two(low)], [two(high), two(low)]])
    sublane = lane.T
    lam = 2.0 - 2.0 * np.cos(np.pi * k / (N + 1))
    diagonal = 2.0 + lam[:, None] + lam[None, :]
    coef = np.zeros((H, N, N))
    coef[0] = 1.0 / diagonal
    for s in range(1, H):
        coef[s] = 1.0 / (diagonal - coef[s - 1])
    middle = 1.0 / (1.0 - coef[-1] ** 2)
    coef = np.concatenate([coef, middle[None]], axis=0)
    coef = np.concatenate([coef, coef], axis=2).reshape((H + 1) * N, L)
    return (
        lane.astype(jnp.bfloat16),
        sublane.astype(jnp.bfloat16),
        coef.astype(np.float32),
    )


def split(x):
    high = x.astype(jnp.bfloat16)
    low = (x - high.astype(jnp.float32)).astype(jnp.bfloat16)
    return high, low


def lane_transform(x, lane_ref):
    high, low = split(x)
    out = jnp.dot(
        jnp.concatenate([high, low], axis=1), lane_ref[...], preferred_element_type=jnp.float32
    )
    return out[:, :L] + out[:, L:]


def sublane_transform(x, sublane_ref):
    high, low = split(x)
    half = 2 * N
    data = jnp.concatenate(
        [
            jnp.concatenate([high[:half], high[half:]], axis=1),
            jnp.concatenate([low[:half], low[half:]], axis=1),
        ],
        axis=0,
    )
    out = jnp.dot(sublane_ref[...], data, preferred_element_type=jnp.float32)
    out = out[:half] + out[half:]
    return jnp.concatenate([out[:, :L], out[:, L:]], axis=0)


def low_lanes(shape):
    return lax.broadcasted_iota(jnp.int32, shape, 1) < N


def tile_rows(t):
    return pl.ds(t * N, N) if isinstance(t, int) else pl.ds(pl.multiple_of(t * N, N), N)


def tile_lanes(t):
    return pl.ds(t * L, L) if isinstance(t, int) else pl.ds(pl.multiple_of(t * L, L), L)


def clear_pads(pad_ref):
    ends = SHIFT + PAD * N
    pad_ref[pl.ds(0, ends), :] = jnp.zeros((ends, L), jnp.float32)
    pad_ref[pl.ds(ends + ROWS, ends), :] = jnp.zeros((ends, L), jnp.float32)


def pad_rows(t):
    start = SHIFT + (PAD + t) * N
    return pl.ds(start if isinstance(t, int) else pl.multiple_of(start, 8), N)


def shifted_reader(pad_ref, displacement, factor):
    da, db, dc = displacement
    flat = db * N + dc
    turn = lax.rem(flat + 16 * L, L)
    jump = lax.div(flat + 16 * L, L) - 16
    lane = lax.broadcasted_iota(jnp.int32, (N, L), 1)
    cell = lane % N + dc
    plane = lax.broadcasted_iota(jnp.int32, (N, L), 0) + da
    inside = (cell >= 0) & (cell < N) & (plane >= 0) & (plane < N)
    weight = jnp.where(inside, factor, 0.0)
    from_next = lane < turn
    back_turn = lax.rem(L - turn, L)

    def read(t):
        start = SHIFT + (PAD + t + jump) * N + da
        here = pad_ref[pl.ds(start, N), :]
        following = pad_ref[pl.ds(start + N, N), :]
        both = jnp.where(from_next, following, here)
        return pltpu.roll(both, back_turn, 1) * weight

    return read


def solve_task(
    refs, i_box, j_box, displacement, factor, times, share, wants_first, wants_second, i_acc, j_acc
):
    (lane_ref, sublane_ref, coef_ref, pad_ref, acc_ref, energy_ref, rj_ref, z_ref) = refs
    low = low_lanes((N, L))

    solves = wants_first or wants_second
    for t in range(H):
        pad_ref[pad_rows(t), :] = j_box[:, tile_lanes(t)].astype(jnp.float32)
    read = shifted_reader(pad_ref, displacement, factor)

    def rows_of(step):
        t = 2 * step
        return (t, t + 1, H - 1 - t, H - 2 - t)

    g = jnp.zeros((N, L), jnp.float32)
    energy = jnp.zeros((8, L), jnp.float32)
    for step in range(H // 4):
        rows = rows_of(step)
        rho = []
        for t in rows:
            seen = read(t)
            phi = i_box[:, tile_lanes(t)].astype(jnp.float32)
            if solves:
                rj_ref[tile_rows(t), :] = seen
                phi = phi * times
            rho.append(phi * seen)
        x = lane_transform(jnp.concatenate(rho, axis=0), lane_ref)
        x = sublane_transform(x, sublane_ref)
        x = [x[k * N : (k + 1) * N] for k in range(4)]
        for k in range(2):
            near, far = x[k], x[2 + k]
            odd = pltpu.roll(jnp.where(low, far, near), N, 1)
            for cell, right in ((2 * rows[k], jnp.where(low, near, far)), (2 * rows[k] + 1, odd)):
                right = right + g
                g = coef_ref[tile_rows(cell), :] * right
                value = g
                if cell == H - 1:
                    value = g + coef_ref[tile_rows(cell), :] * pltpu.roll(g, N, 1)
                    value = value * coef_ref[tile_rows(H), :]
                if solves:
                    z_ref[tile_rows(cell), :] = value
                else:
                    energy = energy + (right * value).reshape(N // 8, 8, L).sum(axis=0)
    if not solves:
        energy_ref[...] += energy * (share * times)
        return

    z = None
    for step in reversed(range(H // 4)):
        rows = rows_of(step)
        x = [None] * 4
        for k in (1, 0):
            t = rows[k]
            odd = z_ref[tile_rows(2 * t + 1), :]
            if z is not None:
                odd = odd + coef_ref[tile_rows(2 * t + 1), :] * z
            z = z_ref[tile_rows(2 * t), :] + coef_ref[tile_rows(2 * t), :] * odd
            turned = pltpu.roll(odd, N, 1)
            x[k] = jnp.where(low, z, turned)
            x[2 + k] = jnp.where(low, turned, z)
        v = sublane_transform(jnp.concatenate(x, axis=0), sublane_ref)
        v = lane_transform(v, lane_ref)
        for k, t in enumerate(rows):
            part = v[k * N : (k + 1) * N]
            phi = i_box[:, tile_lanes(t)].astype(jnp.float32)
            to_first = part * rj_ref[tile_rows(t), :]
            energy = energy + (to_first * phi).reshape(N // 8, 8, L).sum(axis=0)
            if wants_first:
                acc_ref[i_acc, :, tile_lanes(t)] += to_first
            if wants_second:
                pad_ref[pad_rows(t), :] = part * phi
    energy_ref[...] += energy * share
    if wants_second:
        read_back = shifted_reader(pad_ref, [-d for d in displacement], factor)

        for t in range(H):
            acc_ref[j_acc, :, tile_lanes(t)] += read_back(t)


SMEM = pl.BlockSpec(memory_space=pltpu.SMEM)
VMEM = pl.BlockSpec(memory_space=pltpu.VMEM)
HBM = pl.BlockSpec(memory_space=pltpu.HBM)
ANY = pl.BlockSpec(memory_space=pl.ANY)


def stage_kernel(kind, *refs):
    me_ref, offsets_ref, exponents_ref, tables_ref, own_in = refs[:5]
    consts_in, refs = refs[5:8], refs[8:]
    halo_in = earlier_in = energy_in = out_ref = energy_out = None
    if kind != "own":
        halo_in, refs = refs[:2], refs[2:]
    if kind in ("near", "rest"):
        energy_in, refs = refs[0], refs[1:]
    if kind == "far":
        earlier_in, refs = refs[:2], refs[2:]
    if kind != "rest":
        out_ref, refs = refs[0], refs[1:]
    if kind != "far":
        energy_out, refs = refs[0], refs[1:]
    if kind == "own":
        sent, refs = refs[0], refs[1:]
    energy_ref, pad_ref, rj_ref, z_ref, sems, own_ref = refs[:6]
    consts, refs = refs[6:9], refs[9:]
    copies = [(own_in, own_ref)] + list(zip(consts_in, consts))
    if kind != "own":
        halo_ref, refs = refs[0], refs[1:]
        for side in (0, 1):
            for k in range(EARLY):
                box = halo_in[side].at[pl.ds(k * N, N), :]
                copies.append((box, halo_ref.at[side, k]))
    copies = [pltpu.make_async_copy(x, y, sems.at[k]) for k, (x, y) in enumerate(copies)]
    for copy in copies:
        copy.start()
    acc_ref = None
    if kind != "rest":
        acc_ref, refs = refs[0], refs[1:]
    if kind == "far":
        earlier_ref, rounded_ref = refs
        earlier = [
            pltpu.make_async_copy(earlier_in[n], earlier_ref.at[n], sems.at[8 + n]) for n in (0, 1)
        ]
        for copy in earlier:
            copy.start()

    block = own_ref.shape[0]
    groups = exponents_ref.shape[0] // block
    slots = tables_ref.shape[1]
    me = me_ref[0]

    clear_pads(pad_ref)
    energy_ref[...] = jnp.zeros_like(energy_ref) if energy_in is None else energy_in[...]
    if acc_ref is not None:
        acc_ref[...] = jnp.zeros_like(acc_ref)
    for copy in copies:
        copy.wait()
    if kind == "own":
        others = [
            pltpu.make_async_copy(own_ref.at[EARLY + k], sent.at[pl.ds(k * N, N), :], sems.at[4 + k])
            for k in range(block - EARLY)
        ]
        for copy in others:
            copy.start()
    refs = tuple(consts) + (pad_ref, acc_ref, energy_ref, rj_ref, z_ref)

    def power(exponent):
        return jnp.exp2(jnp.full((N, L), exponent, jnp.int32).astype(jnp.float32))

    def run(owner, slot, i_box, j_box, share, wants_first, wants_second):
        row = 0 if kind == "own" else 2 * owner
        local, code = tables_ref[row, slot], tables_ref[row + 1, slot]

        def look(k, found):
            same = ((tables_ref[row, k] == local) & (tables_ref[row + 1, k] == code)).astype(jnp.int32)
            return found[0] + same, found[1] + jnp.where(k < slot, same, 0)

        times, sooner = lax.fori_loop(
            0, slots, look, (jnp.int32(0), jnp.int32(0)), unroll=True
        )

        @pl.when(sooner == 0)
        def _():
            group = me + owner - 1 + groups
            i = lax.rem(group, groups) * block + local
            j = lax.rem((group - 1) * block + code, groups * block)
            solve_task(
                refs,
                i_box,
                j_box,
                [offsets_ref[k, i] - offsets_ref[k, j] for k in range(3)],
                power(exponents_ref[i] + exponents_ref[j]),
                times.astype(jnp.float32),
                jnp.asarray(share).astype(jnp.float32),
                wants_first,
                wants_second,
                local,
                code & (block - 1),
            )

    def in_chunk(local):
        if kind == "near":
            return local < EARLY, jnp.minimum(local, EARLY - 1)
        return local >= EARLY, jnp.maximum(local - EARLY, 0)

    def live_of(row):
        return lax.fori_loop(
            0, slots, lambda k, n: n + (tables_ref[row, k] >= 0).astype(jnp.int32), jnp.int32(0), unroll=True
        )

    wants = kind != "rest"

    def visit_own(slot, carry):
        row = 0 if kind == "own" else 2
        local, code = tables_ref[row, slot], tables_ref[row + 1, slot]
        other, group = code & (block - 1), lax.div(code, block)
        if kind == "own":

            @pl.when(group == 1)
            def _():
                run(1, slot, own_ref.at[local], own_ref.at[other], 1, True, True)

            return carry
        chosen, at = in_chunk(other)
        chosen = chosen & (group != 1)
        side = jnp.where(group == 0, 0, 1)
        if kind == "rest":
            theirs = jnp.where(group == 0, live_before, live_after)
            chosen = chosen & (local >= EARLY) & (live <= theirs)

        @pl.when(chosen)
        def _():
            share = 0 if kind == "far" else 1
            run(1, slot, own_ref.at[local], halo_ref.at[side, at], share, wants, False)

        return carry

    live = live_of(0 if kind == "own" else 2)
    if kind != "own":
        live_before, live_after = live_of(0), live_of(4)
    lax.fori_loop(0, live, visit_own, 0)

    if kind != "own":

        def visit_others(k, carry):
            side = (k >= live_before).astype(jnp.int32)
            slot = k - side * live_before
            local, code = tables_ref[4 * side, slot], tables_ref[4 * side + 1, slot]
            other = code & (block - 1)
            chosen, at = in_chunk(local)
            mine = lax.div(code, block) == 2 - 2 * side
            if kind == "rest":
                theirs = jnp.where(side == 0, live_before, live_after)
                mine = mine & (other >= EARLY) & (live < theirs)

            @pl.when(chosen & mine)
            def _():
                share = {"near": other >= EARLY, "rest": 1, "far": 0}[kind]
                run(2 * side, slot, halo_ref.at[side, at], own_ref.at[other], share, False, wants)

            return carry

        lax.fori_loop(0, live_before + live_after, visit_others, 0)

    if kind == "rest":
        energy_out[...] = jnp.full(energy_out.shape, jnp.sum(energy_ref[...]), jnp.float32)
    elif kind != "far":
        energy_out[...] = energy_ref[...]
    if kind in ("own", "near"):
        copy = pltpu.make_async_copy(acc_ref, out_ref, sems.at[0])
        copy.start()
        copy.wait()
        if kind == "own":
            for copy in others:
                copy.wait()
    if kind == "far":
        for copy in earlier:
            copy.wait()
        for k in range(block):
            scale = -FRACTION * power(-exponents_ref[me * block + k])

            def write(t, carry):
                lanes = tile_lanes(t)
                total = earlier_ref[0, k, :, lanes] + earlier_ref[1, k, :, lanes] + acc_ref[k, :, lanes]
                rounded_ref[k, :, lanes] = (total * scale).astype(jnp.bfloat16)
                return carry

            lax.fori_loop(0, H, write, 0, unroll=4)
            pltpu.make_async_copy(rounded_ref.at[k], out_ref.at[k], sems.at[k]).start()
        for k in range(block):
            pltpu.make_async_copy(rounded_ref.at[k], out_ref.at[k], sems.at[k]).wait()


def stage(kind, peers, scalars, own, consts, halo=(), earlier=(), energy=None):
    totals = jax.ShapeDtypeStruct(own.shape, jnp.float32)
    operands = list(scalars) + [own] + list(consts) + list(halo) + list(earlier)
    specs = [SMEM] * len(scalars) + [ANY] + [HBM] * 3 + [ANY] * len(halo) + [HBM] * len(earlier)
    if energy is not None:
        operands.append(energy)
        specs.append(VMEM)
    out_shapes, out_specs = [], []
    if kind != "rest":
        out_shapes.append(jax.ShapeDtypeStruct(own.shape, own.dtype) if kind == "far" else totals)
        out_specs.append(HBM)
    if kind != "far":
        out_shapes.append(jax.ShapeDtypeStruct((peers if kind == "rest" else 8, L), jnp.float32))
        out_specs.append(VMEM)
    if kind == "own":
        others = (own.shape[0] - EARLY) * own.shape[1]
        out_shapes.append(jax.ShapeDtypeStruct((others, own.shape[2]), own.dtype))
        out_specs.append(HBM)
    scratch = [
        pltpu.VMEM((8, L), jnp.float32),
        pltpu.VMEM(((H + 2 * PAD) * N + 2 * SHIFT, L), jnp.float32),
        pltpu.VMEM((ROWS, L), jnp.float32),
        pltpu.VMEM((ROWS, L), jnp.float32),
        pltpu.SemaphoreType.DMA((10,)),
        pltpu.VMEM(own.shape, own.dtype),
    ] + [pltpu.VMEM(c.shape, c.dtype) for c in consts]
    if halo:
        scratch.append(pltpu.VMEM((2, EARLY) + own.shape[1:], own.dtype))
    if kind != "rest":
        scratch.append(pltpu.VMEM(own.shape, jnp.float32))
    if kind == "far":
        scratch.append(pltpu.VMEM((2,) + own.shape, jnp.float32))
        scratch.append(pltpu.VMEM(own.shape, own.dtype))
    return pl.pallas_call(
        functools.partial(stage_kernel, kind),
        out_shape=out_shapes,
        in_specs=specs,
        out_specs=out_specs,
        scratch_shapes=scratch,
        compiler_params=pltpu.CompilerParams(vmem_limit_bytes=(56 if kind == "far" else 20) * 2**20),
        cost_estimate=pl.CostEstimate(flops=2 * 10**10, bytes_accessed=10**7, transcendentals=0),
    )(*operands)


def on_device(orbitals, exponents, offsets, pair_list):
    own = orbitals[0]
    block, _, width = own.shape
    groups = lax.axis_size("orb")
    peers = groups * lax.axis_size("spin")
    me = lax.axis_index("orb").astype(jnp.int32).reshape(1)
    up = [(k, (k + 1) % groups) for k in range(groups)]
    down = [(k, j) for j, k in up]
    consts = tuple(jnp.asarray(c) for c in tables())

    def exchange(array):
        return lax.ppermute(array, "orb", up), lax.ppermute(array, "orb", down)

    first, second = pair_list[0]
    live = first >= 0
    base = (me - 1) * block
    code = jnp.where(second < base, second + groups * block, second) - base
    code = jnp.where(code >= groups * block, code - groups * block, code)
    table = jnp.stack([jnp.where(live, first - me * block, -1), jnp.where(live, code, -1)])
    listing = jnp.pad(table.astype(own.dtype), ((0, LIST - 2), (0, width - table.shape[1])))
    near = exchange(jnp.concatenate([own[:EARLY].reshape(EARLY * N, width), listing], axis=0))
    rows = slice(EARLY * N, EARLY * N + 2)
    lists = [x[rows, : table.shape[1]].astype(jnp.int32) for x in near]
    around = jnp.concatenate([lists[0], table, lists[1]], axis=0)

    scalars = (me, offsets[0], exponents[0])
    acc, energy, others = stage("own", peers, scalars + (table,), own, consts)
    far = exchange(others)
    scalars += (around,)
    more, energy = stage("near", peers, scalars, own, consts, near, energy=energy)
    (rows,) = stage("rest", peers, scalars, own, consts, far, energy=energy)
    rows = lax.all_to_all(rows, ("spin", "orb"), 0, 0)
    (potentials,) = stage("far", peers, scalars, own, consts, far, (acc, more))
    return (potentials[None], -FRACTION / N**3 * jnp.sum(rows[:, 0]))


def solution(mesh):
    in_specs = (
        P("spin", "orb", None, None),
        P("spin", None),
        P("spin", None, None),
        P("spin", None, "orb"),
    )
    out_specs = (P("spin", "orb", None, None), P())
    return jax.shard_map(
        on_device, mesh=mesh, in_specs=in_specs, out_specs=out_specs, check_vma=False
    )
```

```python
import functools

import jax
import jax.numpy as jnp
import numpy as np
from jax import lax
from jax.experimental import pallas as pl
from jax.experimental.pallas import tpu as pltpu
from jax.sharding import PartitionSpec as P

FRACTION = 0.25
N = 64
H = N // 2
L = 2 * N
SHIFT = 16
PAD = SHIFT // 2 + 1
ROWS = H * N
EARLY = 2
LIST = 16


def split_np(matrix):
    high = matrix.astype(jnp.bfloat16).astype(np.float64)
    low = (matrix - high).astype(jnp.bfloat16).astype(np.float64)
    return high, low


def tables():
    k = np.arange(N, dtype=np.float64) + 1.0
    sine = np.sqrt(2.0 / (N + 1)) * np.sin(np.pi * k[:, None] * k[None, :] / (N + 1))
    high, low = split_np(sine)
    two = lambda m: np.kron(np.eye(2), m)
    lane = np.block([[two(high), two(low)], [two(high), two(low)]])
    sublane = lane.T
    lam = 2.0 - 2.0 * np.cos(np.pi * k / (N + 1))
    diagonal = 2.0 + lam[:, None] + lam[None, :]
    coef = np.zeros((H, N, N))
    coef[0] = 1.0 / diagonal
    for s in range(1, H):
        coef[s] = 1.0 / (diagonal - coef[s - 1])
    middle = 1.0 / (1.0 - coef[-1] ** 2)
    coef = np.concatenate([coef, middle[None]], axis=0)
    coef = np.concatenate([coef, coef], axis=2).reshape((H + 1) * N, L)
    return (
        lane.astype(jnp.bfloat16),
        sublane.astype(jnp.bfloat16),
        coef.astype(np.float32),
    )


def split(x):
    high = x.astype(jnp.bfloat16)
    low = (x - high.astype(jnp.float32)).astype(jnp.bfloat16)
    return high, low


def lane_transform(x, lane_ref):
    high, low = split(x)
    out = jnp.dot(
        jnp.concatenate([high, low], axis=1), lane_ref[...], preferred_element_type=jnp.float32
    )
    return out[:, :L] + out[:, L:]


def sublane_transform(x, sublane_ref):
    high, low = split(x)
    half = 2 * N
    data = jnp.concatenate(
        [
            jnp.concatenate([high[:half], high[half:]], axis=1),
            jnp.concatenate([low[:half], low[half:]], axis=1),
        ],
        axis=0,
    )
    out = jnp.dot(sublane_ref[...], data, preferred_element_type=jnp.float32)
    out = out[:half] + out[half:]
    return jnp.concatenate([out[:, :L], out[:, L:]], axis=0)


def low_lanes(shape):
    return lax.broadcasted_iota(jnp.int32, shape, 1) < N


def tile_rows(t):
    return pl.ds(t * N, N) if isinstance(t, int) else pl.ds(pl.multiple_of(t * N, N), N)


def tile_lanes(t):
    return pl.ds(t * L, L) if isinstance(t, int) else pl.ds(pl.multiple_of(t * L, L), L)


def clear_pads(pad_ref):
    ends = SHIFT + PAD * N
    pad_ref[pl.ds(0, ends), :] = jnp.zeros((ends, L), jnp.float32)
    pad_ref[pl.ds(ends + ROWS, ends), :] = jnp.zeros((ends, L), jnp.float32)


def pad_rows(t):
    start = SHIFT + (PAD + t) * N
    return pl.ds(start if isinstance(t, int) else pl.multiple_of(start, 8), N)


def shifted_reader(pad_ref, displacement, factor):
    da, db, dc = displacement
    flat = db * N + dc
    turn = lax.rem(flat + 16 * L, L)
    jump = lax.div(flat + 16 * L, L) - 16
    lane = lax.broadcasted_iota(jnp.int32, (N, L), 1)
    cell = lane % N + dc
    plane = lax.broadcasted_iota(jnp.int32, (N, L), 0) + da
    inside = (cell >= 0) & (cell < N) & (plane >= 0) & (plane < N)
    weight = jnp.where(inside, factor, 0.0)
    from_next = lane < turn
    back_turn = lax.rem(L - turn, L)

    def read(t):
        start = SHIFT + (PAD + t + jump) * N + da
        here = pad_ref[pl.ds(start, N), :]
        following = pad_ref[pl.ds(start + N, N), :]
        both = jnp.where(from_next, following, here)
        return pltpu.roll(both, back_turn, 1) * weight

    return read


def solve_task(
    refs, i_box, j_box, displacement, factor, times, share, wants_first, wants_second, i_acc, j_acc, counts
):
    (lane_ref, sublane_ref, coef_ref, pad_ref, acc_ref, energy_ref, rj_ref, z_ref) = refs
    low = low_lanes((N, L))

    solves = wants_first or wants_second
    for t in range(H):
        pad_ref[pad_rows(t), :] = j_box[:, tile_lanes(t)].astype(jnp.float32)
    read = shifted_reader(pad_ref, displacement, factor)

    def rows_of(step):
        t = 2 * step
        return (t, t + 1, H - 1 - t, H - 2 - t)

    g = jnp.zeros((N, L), jnp.float32)
    energy = jnp.zeros((8, L), jnp.float32)
    for step in range(H // 4):
        rows = rows_of(step)
        rho = []
        for t in rows:
            seen = read(t)
            phi = i_box[:, tile_lanes(t)].astype(jnp.float32)
            if solves:
                rj_ref[tile_rows(t), :] = seen
                phi = phi * times
            rho.append(phi * seen)
        x = lane_transform(jnp.concatenate(rho, axis=0), lane_ref)
        x = sublane_transform(x, sublane_ref)
        x = [x[k * N : (k + 1) * N] for k in range(4)]
        for k in range(2):
            near, far = x[k], x[2 + k]
            odd = pltpu.roll(jnp.where(low, far, near), N, 1)
            for cell, right in ((2 * rows[k], jnp.where(low, near, far)), (2 * rows[k] + 1, odd)):
                right = right + g
                g = coef_ref[tile_rows(cell), :] * right
                value = g
                if cell == H - 1:
                    value = g + coef_ref[tile_rows(cell), :] * pltpu.roll(g, N, 1)
                    value = value * coef_ref[tile_rows(H), :]
                if solves:
                    z_ref[tile_rows(cell), :] = value
                else:
                    energy = energy + (right * value).reshape(N // 8, 8, L).sum(axis=0)
    if not solves:
        energy_ref[...] += energy * (share * times)
        return

    z = None
    for step in reversed(range(H // 4)):
        rows = rows_of(step)
        x = [None] * 4
        for k in (1, 0):
            t = rows[k]
            odd = z_ref[tile_rows(2 * t + 1), :]
            if z is not None:
                odd = odd + coef_ref[tile_rows(2 * t + 1), :] * z
            z = z_ref[tile_rows(2 * t), :] + coef_ref[tile_rows(2 * t), :] * odd
            turned = pltpu.roll(odd, N, 1)
            x[k] = jnp.where(low, z, turned)
            x[2 + k] = jnp.where(low, turned, z)
        v = sublane_transform(jnp.concatenate(x, axis=0), sublane_ref)
        v = lane_transform(v, lane_ref)
        for k, t in enumerate(rows):
            part = v[k * N : (k + 1) * N]
            phi = i_box[:, tile_lanes(t)].astype(jnp.float32)
            to_first = part * rj_ref[tile_rows(t), :]
            if counts:
                energy = energy + (to_first * phi).reshape(N // 8, 8, L).sum(axis=0)
            if wants_first:
                acc_ref[i_acc, :, tile_lanes(t)] += to_first
            if wants_second:
                pad_ref[pad_rows(t), :] = part * phi
    if counts:
        energy_ref[...] += energy * share
    if wants_second:
        read_back = shifted_reader(pad_ref, [-d for d in displacement], factor)

        for t in range(H):
            acc_ref[j_acc, :, tile_lanes(t)] += read_back(t)


SMEM = pl.BlockSpec(memory_space=pltpu.SMEM)
VMEM = pl.BlockSpec(memory_space=pltpu.VMEM)
HBM = pl.BlockSpec(memory_space=pltpu.HBM)
ANY = pl.BlockSpec(memory_space=pl.ANY)


def stage_kernel(kind, *refs):
    me_ref, offsets_ref, exponents_ref, tables_ref, own_in = refs[:5]
    consts_in, refs = refs[5:8], refs[8:]
    halo_in = earlier_in = energy_in = out_ref = energy_out = None
    if kind != "own":
        halo_in, refs = refs[:2], refs[2:]
    if kind == "near":
        acc_in, refs = refs[0], refs[1:]
    if kind in ("near", "rest"):
        energy_in, refs = refs[0], refs[1:]
    if kind == "far":
        earlier_in, refs = refs[0], refs[1:]
    if kind != "rest":
        out_ref, refs = refs[0], refs[1:]
    if kind != "far":
        energy_out, refs = refs[0], refs[1:]
    if kind == "own":
        sent, refs = refs[0], refs[1:]
    energy_ref, pad_ref, rj_ref, z_ref, sems, own_ref = refs[:6]
    consts, refs = refs[6:9], refs[9:]
    copies = [(own_in, own_ref)] + list(zip(consts_in, consts))
    if kind != "own":
        halo_ref, refs = refs[0], refs[1:]
        for side in (0, 1):
            for k in range(EARLY):
                box = halo_in[side].at[pl.ds(k * N, N), :]
                copies.append((box, halo_ref.at[side, k]))
    copies = [pltpu.make_async_copy(x, y, sems.at[k]) for k, (x, y) in enumerate(copies)]
    for copy in copies:
        copy.start()
    acc_ref = None
    if kind != "rest":
        acc_ref, refs = refs[0], refs[1:]
    if kind == "near":
        copies.append(pltpu.make_async_copy(acc_in, acc_ref, sems.at[8]))
        copies[-1].start()
    if kind == "far":
        earlier_ref, rounded_ref = refs
        earlier = pltpu.make_async_copy(earlier_in, earlier_ref, sems.at[8])
        earlier.start()

    block = own_ref.shape[0]
    groups = exponents_ref.shape[0] // block
    slots = tables_ref.shape[1]
    me = me_ref[0]

    clear_pads(pad_ref)
    energy_ref[...] = jnp.zeros_like(energy_ref) if energy_in is None else energy_in[...]
    if kind in ("own", "far"):
        acc_ref[...] = jnp.zeros_like(acc_ref)
    for copy in copies:
        copy.wait()
    if kind == "own":
        others = [
            pltpu.make_async_copy(own_ref.at[EARLY + k], sent.at[pl.ds(k * N, N), :], sems.at[4 + k])
            for k in range(block - EARLY)
        ]
        for copy in others:
            copy.start()
    refs = tuple(consts) + (pad_ref, acc_ref, energy_ref, rj_ref, z_ref)

    def power(exponent):
        return jnp.exp2(jnp.full((N, L), exponent, jnp.int32).astype(jnp.float32))

    def two_to(exponent):
        below = jnp.where(exponent < -1, 0.25, 0.5)
        above = jnp.where(exponent > 1, 4.0, 2.0)
        return jnp.where(exponent < 0, below, jnp.where(exponent > 0, above, 1.0)).astype(jnp.float32)

    def run(owner, slot, i_box, j_box, share, wants_first, wants_second):
        row = 0 if kind == "own" else 2 * owner
        local, code = tables_ref[row, slot], tables_ref[row + 1, slot]

        def look(k, found):
            same = ((tables_ref[row, k] == local) & (tables_ref[row + 1, k] == code)).astype(jnp.int32)
            return found[0] + same, found[1] + jnp.where(k < slot, same, 0)

        times, sooner = lax.fori_loop(
            0, slots, look, (jnp.int32(0), jnp.int32(0)), unroll=True
        )

        @pl.when(sooner == 0)
        def _():
            group = me + owner - 1 + groups
            i = lax.rem(group, groups) * block + local
            j = lax.rem((group - 1) * block + code, groups * block)
            solve_task(
                refs,
                i_box,
                j_box,
                [offsets_ref[k, i] - offsets_ref[k, j] for k in range(3)],
                two_to(exponents_ref[i] + exponents_ref[j]),
                times.astype(jnp.float32),
                jnp.asarray(share).astype(jnp.float32),
                wants_first,
                wants_second,
                local,
                code & (block - 1),
                kind != "far",
            )

    def in_chunk(local):
        if kind == "near":
            return local < EARLY, jnp.minimum(local, EARLY - 1)
        return local >= EARLY, jnp.maximum(local - EARLY, 0)

    def live_of(row):
        return lax.fori_loop(
            0, slots, lambda k, n: n + (tables_ref[row, k] >= 0).astype(jnp.int32), jnp.int32(0), unroll=True
        )

    wants = kind != "rest"

    def visit_own(slot, carry):
        row = 0 if kind == "own" else 2
        local, code = tables_ref[row, slot], tables_ref[row + 1, slot]
        other, group = code & (block - 1), lax.div(code, block)
        if kind == "own":

            @pl.when(group == 1)
            def _():
                run(1, slot, own_ref.at[local], own_ref.at[other], 1, True, True)

            return carry
        chosen, at = in_chunk(other)
        chosen = chosen & (group != 1)
        side = jnp.where(group == 0, 0, 1)
        if kind == "rest":
            theirs = jnp.where(group == 0, live_before, live_after)
            chosen = chosen & (local >= EARLY) & (live <= theirs)

        @pl.when(chosen)
        def _():
            share = 0 if kind == "far" else 1
            run(1, slot, own_ref.at[local], halo_ref.at[side, at], share, wants, False)

        return carry

    live = live_of(0 if kind == "own" else 2)
    if kind != "own":
        live_before, live_after = live_of(0), live_of(4)
    lax.fori_loop(0, live, visit_own, 0)

    if kind != "own":

        def visit_others(k, carry):
            side = (k >= live_before).astype(jnp.int32)
            slot = k - side * live_before
            local, code = tables_ref[4 * side, slot], tables_ref[4 * side + 1, slot]
            other = code & (block - 1)
            chosen, at = in_chunk(local)
            mine = lax.div(code, block) == 2 - 2 * side
            if kind == "rest":
                theirs = jnp.where(side == 0, live_before, live_after)
                mine = mine & (other >= EARLY) & (live < theirs)

            @pl.when(chosen & mine)
            def _():
                share = {"near": other >= EARLY, "rest": 1, "far": 0}[kind]
                run(2 * side, slot, halo_ref.at[side, at], own_ref.at[other], share, False, wants)

            return carry

        lax.fori_loop(0, live_before + live_after, visit_others, 0)

    if kind == "rest":
        energy_out[...] = jnp.full(energy_out.shape, jnp.sum(energy_ref[...]), jnp.float32)
    elif kind != "far":
        energy_out[...] = energy_ref[...]
    if kind in ("own", "near"):
        copy = pltpu.make_async_copy(acc_ref, out_ref, sems.at[0])
        copy.start()
        copy.wait()
        if kind == "own":
            for copy in others:
                copy.wait()
    if kind == "far":
        earlier.wait()
        for k in range(block):
            scale = -FRACTION * power(-exponents_ref[me * block + k])

            def write(t, carry):
                lanes = tile_lanes(t)
                total = earlier_ref[k, :, lanes] + acc_ref[k, :, lanes]
                rounded_ref[k, :, lanes] = (total * scale).astype(jnp.bfloat16)
                return carry

            lax.fori_loop(0, H, write, 0, unroll=4)
            pltpu.make_async_copy(rounded_ref.at[k], out_ref.at[k], sems.at[k]).start()
        for k in range(block):
            pltpu.make_async_copy(rounded_ref.at[k], out_ref.at[k], sems.at[k]).wait()


def stage(kind, peers, scalars, own, consts, halo=(), earlier=None, energy=None):
    totals = jax.ShapeDtypeStruct(own.shape, jnp.float32)
    operands = list(scalars) + [own] + list(consts) + list(halo)
    specs = [SMEM] * len(scalars) + [ANY] + [HBM] * 3 + [ANY] * len(halo)
    if earlier is not None:
        operands.append(earlier)
        specs.append(HBM if kind == "far" else ANY)
    if energy is not None:
        operands.append(energy)
        specs.append(VMEM)
    out_shapes, out_specs = [], []
    if kind != "rest":
        out_shapes.append(jax.ShapeDtypeStruct(own.shape, own.dtype) if kind == "far" else totals)
        out_specs.append(ANY if kind == "own" else HBM)
    if kind != "far":
        out_shapes.append(jax.ShapeDtypeStruct((peers if kind == "rest" else 8, L), jnp.float32))
        out_specs.append(VMEM)
    if kind == "own":
        others = (own.shape[0] - EARLY) * own.shape[1]
        out_shapes.append(jax.ShapeDtypeStruct((others, own.shape[2]), own.dtype))
        out_specs.append(HBM)
    scratch = [
        pltpu.VMEM((8, L), jnp.float32),
        pltpu.VMEM(((H + 2 * PAD) * N + 2 * SHIFT, L), jnp.float32),
        pltpu.VMEM((ROWS, L), jnp.float32),
        pltpu.VMEM((ROWS, L), jnp.float32),
        pltpu.SemaphoreType.DMA((10,)),
        pltpu.VMEM(own.shape, own.dtype),
    ] + [pltpu.VMEM(c.shape, c.dtype) for c in consts]
    if halo:
        scratch.append(pltpu.VMEM((2, EARLY) + own.shape[1:], own.dtype))
    if kind != "rest":
        scratch.append(pltpu.VMEM(own.shape, jnp.float32))
    if kind == "far":
        scratch.append(pltpu.VMEM(own.shape, jnp.float32))
        scratch.append(pltpu.VMEM(own.shape, own.dtype))
    return pl.pallas_call(
        functools.partial(stage_kernel, kind),
        out_shape=out_shapes,
        in_specs=specs,
        out_specs=out_specs,
        scratch_shapes=scratch,
        compiler_params=pltpu.CompilerParams(vmem_limit_bytes=(56 if kind == "far" else 20) * 2**20),
        cost_estimate=pl.CostEstimate(flops=2 * 10**10, bytes_accessed=10**7, transcendentals=0),
    )(*operands)


def on_device(orbitals, exponents, offsets, pair_list):
    own = orbitals[0]
    block, _, width = own.shape
    groups = lax.axis_size("orb")
    peers = groups * lax.axis_size("spin")
    me = lax.axis_index("orb").astype(jnp.int32).reshape(1)
    up = [(k, (k + 1) % groups) for k in range(groups)]
    down = [(k, j) for j, k in up]
    consts = tuple(jnp.asarray(c) for c in tables())

    def exchange(array):
        return lax.ppermute(array, "orb", up), lax.ppermute(array, "orb", down)

    first, second = pair_list[0]
    live = first >= 0
    base = (me - 1) * block
    code = jnp.where(second < base, second + groups * block, second) - base
    code = jnp.where(code >= groups * block, code - groups * block, code)
    table = jnp.stack([jnp.where(live, first - me * block, -1), jnp.where(live, code, -1)])
    listing = jnp.pad(table.astype(own.dtype), ((0, LIST - 2), (0, width - table.shape[1])))
    near = exchange(jnp.concatenate([own[:EARLY].reshape(EARLY * N, width), listing], axis=0))
    rows = slice(EARLY * N, EARLY * N + 2)
    lists = [x[rows, : table.shape[1]].astype(jnp.int32) for x in near]
    around = jnp.concatenate([lists[0], table, lists[1]], axis=0)

    scalars = (me, offsets[0], exponents[0])
    acc, energy, others = stage("own", peers, scalars + (table,), own, consts)
    far = exchange(others)
    scalars += (around,)
    acc, energy = stage("near", peers, scalars, own, consts, near, acc, energy)
    (rows,) = stage("rest", peers, scalars, own, consts, far, energy=energy)
    rows = lax.all_to_all(rows, ("spin", "orb"), 0, 0)
    (potentials,) = stage("far", peers, scalars, own, consts, far, acc)
    return (potentials[None], -FRACTION / N**3 * jnp.sum(rows[:, 0]))


def solution(mesh):
    in_specs = (
        P("spin", "orb", None, None),
        P("spin", None),
        P("spin", None, None),
        P("spin", None, "orb"),
    )
    out_specs = (P("spin", "orb", None, None), P())
    return jax.shard_map(
        on_device, mesh=mesh, in_specs=in_specs, out_specs=out_specs, check_vma=False
    )
```

```python
import functools

import jax
import jax.numpy as jnp
import numpy as np
from jax import lax
from jax.experimental import pallas as pl
from jax.experimental.pallas import tpu as pltpu
from jax.sharding import PartitionSpec as P

FRACTION = 0.25
N = 64
H = N // 2
L = 2 * N
SHIFT = 16
PAD = SHIFT // 2 + 1
ROWS = H * N
CHUNKS = {"near": (0, 2), "mid": (2, 1), "far": (3, 1), "rest": (3, 1)}
LAST = 3
LIST = 16


def split_np(matrix):
    high = matrix.astype(jnp.bfloat16).astype(np.float64)
    low = (matrix - high).astype(jnp.bfloat16).astype(np.float64)
    return high, low


def tables():
    k = np.arange(N, dtype=np.float64) + 1.0
    sine = np.sqrt(2.0 / (N + 1)) * np.sin(np.pi * k[:, None] * k[None, :] / (N + 1))
    high, low = split_np(sine)
    two = lambda m: np.kron(np.eye(2), m)
    lane = np.block([[two(high), two(low)], [two(high), two(low)]])
    sublane = lane.T
    lam = 2.0 - 2.0 * np.cos(np.pi * k / (N + 1))
    diagonal = 2.0 + lam[:, None] + lam[None, :]
    coef = np.zeros((H, N, N))
    coef[0] = 1.0 / diagonal
    for s in range(1, H):
        coef[s] = 1.0 / (diagonal - coef[s - 1])
    middle = 1.0 / (1.0 - coef[-1] ** 2)
    coef = np.concatenate([coef, middle[None]], axis=0)
    coef = np.concatenate([coef, coef], axis=2).reshape((H + 1) * N, L)
    return (
        lane.astype(jnp.bfloat16),
        sublane.astype(jnp.bfloat16),
        coef.astype(np.float32),
    )


def split(x):
    high = x.astype(jnp.bfloat16)
    low = (x - high.astype(jnp.float32)).astype(jnp.bfloat16)
    return high, low


def lane_transform(x, lane_ref):
    high, low = split(x)
    out = jnp.dot(
        jnp.concatenate([high, low], axis=1), lane_ref[...], preferred_element_type=jnp.float32
    )
    return out[:, :L] + out[:, L:]


def sublane_transform(x, sublane_ref):
    high, low = split(x)
    half = 2 * N
    data = jnp.concatenate(
        [
            jnp.concatenate([high[:half], high[half:]], axis=1),
            jnp.concatenate([low[:half], low[half:]], axis=1),
        ],
        axis=0,
    )
    out = jnp.dot(sublane_ref[...], data, preferred_element_type=jnp.float32)
    out = out[:half] + out[half:]
    return jnp.concatenate([out[:, :L], out[:, L:]], axis=0)


def low_lanes(shape):
    return lax.broadcasted_iota(jnp.int32, shape, 1) < N


def tile_rows(t):
    return pl.ds(t * N, N) if isinstance(t, int) else pl.ds(pl.multiple_of(t * N, N), N)


def tile_lanes(t):
    return pl.ds(t * L, L) if isinstance(t, int) else pl.ds(pl.multiple_of(t * L, L), L)


def clear_pads(pad_ref):
    ends = SHIFT + PAD * N
    pad_ref[pl.ds(0, ends), :] = jnp.zeros((ends, L), jnp.float32)
    pad_ref[pl.ds(ends + ROWS, ends), :] = jnp.zeros((ends, L), jnp.float32)


def pad_rows(t):
    start = SHIFT + (PAD + t) * N
    return pl.ds(start if isinstance(t, int) else pl.multiple_of(start, 8), N)


def shifted_reader(pad_ref, displacement, factor):
    da, db, dc = displacement
    flat = db * N + dc
    turn = lax.rem(flat + 16 * L, L)
    jump = lax.div(flat + 16 * L, L) - 16
    lane = lax.broadcasted_iota(jnp.int32, (N, L), 1)
    cell = lane % N + dc
    plane = lax.broadcasted_iota(jnp.int32, (N, L), 0) + da
    inside = (cell >= 0) & (cell < N) & (plane >= 0) & (plane < N)
    weight = jnp.where(inside, factor, 0.0)
    from_next = lane < turn
    back_turn = lax.rem(L - turn, L)

    def read(t):
        start = SHIFT + (PAD + t + jump) * N + da
        here = pad_ref[pl.ds(start, N), :]
        following = pad_ref[pl.ds(start + N, N), :]
        both = jnp.where(from_next, following, here)
        return pltpu.roll(both, back_turn, 1) * weight

    return read


def solve_task(
    refs, i_box, j_box, displacement, factor, times, share, wants_first, wants_second, i_acc, j_acc, counts
):
    (lane_ref, sublane_ref, coef_ref, pad_ref, acc_ref, energy_ref, rj_ref, z_ref) = refs
    low = low_lanes((N, L))

    solves = wants_first or wants_second
    for t in range(H):
        pad_ref[pad_rows(t), :] = j_box[:, tile_lanes(t)].astype(jnp.float32)
    read = shifted_reader(pad_ref, displacement, factor)

    def rows_of(step):
        t = 2 * step
        return (t, t + 1, H - 1 - t, H - 2 - t)

    g = jnp.zeros((N, L), jnp.float32)
    energy = jnp.zeros((8, L), jnp.float32)
    for step in range(H // 4):
        rows = rows_of(step)
        rho = []
        for t in rows:
            seen = read(t)
            phi = i_box[:, tile_lanes(t)].astype(jnp.float32)
            if solves:
                rj_ref[tile_rows(t), :] = seen
                phi = phi * times
            rho.append(phi * seen)
        x = lane_transform(jnp.concatenate(rho, axis=0), lane_ref)
        x = sublane_transform(x, sublane_ref)
        x = [x[k * N : (k + 1) * N] for k in range(4)]
        for k in range(2):
            near, far = x[k], x[2 + k]
            odd = pltpu.roll(jnp.where(low, far, near), N, 1)
            for cell, right in ((2 * rows[k], jnp.where(low, near, far)), (2 * rows[k] + 1, odd)):
                right = right + g
                g = coef_ref[tile_rows(cell), :] * right
                value = g
                if cell == H - 1:
                    value = g + coef_ref[tile_rows(cell), :] * pltpu.roll(g, N, 1)
                    value = value * coef_ref[tile_rows(H), :]
                if solves:
                    z_ref[tile_rows(cell), :] = value
                else:
                    energy = energy + (right * value).reshape(N // 8, 8, L).sum(axis=0)
    if not solves:
        energy_ref[...] += energy * (share * times)
        return

    z = None
    for step in reversed(range(H // 4)):
        rows = rows_of(step)
        x = [None] * 4
        for k in (1, 0):
            t = rows[k]
            odd = z_ref[tile_rows(2 * t + 1), :]
            if z is not None:
                odd = odd + coef_ref[tile_rows(2 * t + 1), :] * z
            z = z_ref[tile_rows(2 * t), :] + coef_ref[tile_rows(2 * t), :] * odd
            turned = pltpu.roll(odd, N, 1)
            x[k] = jnp.where(low, z, turned)
            x[2 + k] = jnp.where(low, turned, z)
        v = sublane_transform(jnp.concatenate(x, axis=0), sublane_ref)
        v = lane_transform(v, lane_ref)
        for k, t in enumerate(rows):
            part = v[k * N : (k + 1) * N]
            phi = i_box[:, tile_lanes(t)].astype(jnp.float32)
            to_first = part * rj_ref[tile_rows(t), :]
            if counts:
                energy = energy + (to_first * phi).reshape(N // 8, 8, L).sum(axis=0)
            if wants_first:
                acc_ref[i_acc, :, tile_lanes(t)] += to_first
            if wants_second:
                pad_ref[pad_rows(t), :] = part * phi
    if counts:
        energy_ref[...] += energy * share
    if wants_second:
        read_back = shifted_reader(pad_ref, [-d for d in displacement], factor)

        for t in range(H):
            acc_ref[j_acc, :, tile_lanes(t)] += read_back(t)


SMEM = pl.BlockSpec(memory_space=pltpu.SMEM)
VMEM = pl.BlockSpec(memory_space=pltpu.VMEM)
HBM = pl.BlockSpec(memory_space=pltpu.HBM)
ANY = pl.BlockSpec(memory_space=pl.ANY)


def stage_kernel(kind, *refs):
    first, count = CHUNKS.get(kind, (0, 0))
    me_ref, offsets_ref, exponents_ref, tables_ref, own_in = refs[:5]
    consts_in, refs = refs[5:8], refs[8:]
    halo_in = earlier_in = energy_in = out_ref = energy_out = None
    if kind != "own":
        halo_in, refs = refs[:2], refs[2:]
    if kind in ("near", "mid"):
        acc_in, refs = refs[0], refs[1:]
    if kind in ("near", "mid", "rest"):
        energy_in, refs = refs[0], refs[1:]
    if kind == "far":
        earlier_in, refs = refs[0], refs[1:]
    if kind != "rest":
        out_ref, refs = refs[0], refs[1:]
    if kind != "far":
        energy_out, refs = refs[0], refs[1:]
    if kind == "own":
        sent, refs = refs[:2], refs[2:]
    energy_ref, pad_ref, rj_ref, z_ref, sems, own_ref = refs[:6]
    consts, refs = refs[6:9], refs[9:]
    copies = [(own_in, own_ref)] + list(zip(consts_in, consts))
    if kind != "own":
        halo_ref, refs = refs[0], refs[1:]
        for side in (0, 1):
            for k in range(count):
                box = halo_in[side].at[pl.ds(k * N, N), :]
                copies.append((box, halo_ref.at[side, k]))
    copies = [pltpu.make_async_copy(x, y, sems.at[k]) for k, (x, y) in enumerate(copies)]
    for copy in copies:
        copy.start()
    acc_ref = None
    if kind != "rest":
        acc_ref, refs = refs[0], refs[1:]
    if kind in ("near", "mid"):
        copies.append(pltpu.make_async_copy(acc_in, acc_ref, sems.at[8]))
        copies[-1].start()
    if kind == "far":
        earlier_ref, rounded_ref = refs
        earlier = pltpu.make_async_copy(earlier_in, earlier_ref, sems.at[8])
        earlier.start()

    block = own_ref.shape[0]
    groups = exponents_ref.shape[0] // block
    slots = tables_ref.shape[1]
    me = me_ref[0]

    clear_pads(pad_ref)
    energy_ref[...] = jnp.zeros_like(energy_ref) if energy_in is None else energy_in[...]
    if kind in ("own", "far"):
        acc_ref[...] = jnp.zeros_like(acc_ref)
    for copy in copies:
        copy.wait()
    if kind == "own":
        others = [
            pltpu.make_async_copy(own_ref.at[k], sent[n], sems.at[4 + n])
            for n, k in enumerate((CHUNKS["mid"][0], LAST))
        ]
        for copy in others:
            copy.start()
    refs = tuple(consts) + (pad_ref, acc_ref, energy_ref, rj_ref, z_ref)

    def power(exponent):
        return jnp.exp2(jnp.full((N, L), exponent, jnp.int32).astype(jnp.float32))

    def two_to(exponent):
        below = jnp.where(exponent < -1, 0.25, 0.5)
        above = jnp.where(exponent > 1, 4.0, 2.0)
        return jnp.where(exponent < 0, below, jnp.where(exponent > 0, above, 1.0)).astype(jnp.float32)

    def run(owner, slot, i_box, j_box, share, wants_first, wants_second):
        row = 0 if kind == "own" else 2 * owner
        local, code = tables_ref[row, slot], tables_ref[row + 1, slot]

        def look(k, found):
            same = ((tables_ref[row, k] == local) & (tables_ref[row + 1, k] == code)).astype(jnp.int32)
            return found[0] + same, found[1] + jnp.where(k < slot, same, 0)

        times, sooner = lax.fori_loop(
            0, slots, look, (jnp.int32(0), jnp.int32(0)), unroll=True
        )

        @pl.when(sooner == 0)
        def _():
            group = me + owner - 1 + groups
            i = lax.rem(group, groups) * block + local
            j = lax.rem((group - 1) * block + code, groups * block)
            solve_task(
                refs,
                i_box,
                j_box,
                [offsets_ref[k, i] - offsets_ref[k, j] for k in range(3)],
                two_to(exponents_ref[i] + exponents_ref[j]),
                times.astype(jnp.float32),
                jnp.asarray(share).astype(jnp.float32),
                wants_first,
                wants_second,
                local,
                code & (block - 1),
                kind != "far",
            )

    def in_chunk(local):
        place = local - first
        return (place >= 0) & (place < count), jnp.clip(place, 0, count - 1)

    def live_of(row):
        return lax.fori_loop(
            0, slots, lambda k, n: n + (tables_ref[row, k] >= 0).astype(jnp.int32), jnp.int32(0), unroll=True
        )

    wants = kind != "rest"

    def visit_own(slot, carry):
        row = 0 if kind == "own" else 2
        local, code = tables_ref[row, slot], tables_ref[row + 1, slot]
        other, group = code & (block - 1), lax.div(code, block)
        if kind == "own":

            @pl.when(group == 1)
            def _():
                run(1, slot, own_ref.at[local], own_ref.at[other], 1, True, True)

            return carry
        chosen, at = in_chunk(other)
        chosen = chosen & (group != 1)
        side = jnp.where(group == 0, 0, 1)
        if kind == "rest":
            theirs = jnp.where(group == 0, live_before, live_after)
            chosen = chosen & (local == LAST) & (live <= theirs)

        @pl.when(chosen)
        def _():
            share = {"own": 1, "near": 1, "mid": local >= first, "far": 0, "rest": 1}[kind]
            run(1, slot, own_ref.at[local], halo_ref.at[side, at], share, wants, False)

        return carry

    live = live_of(0 if kind == "own" else 2)
    if kind != "own":
        live_before, live_after = live_of(0), live_of(4)
    lax.fori_loop(0, live, visit_own, 0)

    if kind != "own":

        def visit_others(k, carry):
            side = (k >= live_before).astype(jnp.int32)
            slot = k - side * live_before
            local, code = tables_ref[4 * side, slot], tables_ref[4 * side + 1, slot]
            other = code & (block - 1)
            chosen, at = in_chunk(local)
            mine = lax.div(code, block) == 2 - 2 * side
            if kind == "rest":
                theirs = jnp.where(side == 0, live_before, live_after)
                mine = mine & (other == LAST) & (live < theirs)

            @pl.when(chosen & mine)
            def _():
                share = {"near": other >= first + count, "mid": other == LAST, "rest": 1, "far": 0}[kind]
                run(2 * side, slot, halo_ref.at[side, at], own_ref.at[other], share, False, wants)

            return carry

        lax.fori_loop(0, live_before + live_after, visit_others, 0)

    if kind == "rest":
        energy_out[...] = jnp.full(
            energy_out.shape, -FRACTION / N**3 * jnp.sum(energy_ref[...]), jnp.float32
        )
    elif kind != "far":
        energy_out[...] = energy_ref[...]
    if kind in ("own", "near", "mid"):
        copy = pltpu.make_async_copy(acc_ref, out_ref, sems.at[0])
        copy.start()
        copy.wait()
        if kind == "own":
            for copy in others:
                copy.wait()
    if kind == "far":
        earlier.wait()
        for k in range(block):
            scale = -FRACTION * power(-exponents_ref[me * block + k])

            def write(t, carry):
                lanes = tile_lanes(t)
                total = earlier_ref[k, :, lanes] + acc_ref[k, :, lanes]
                rounded_ref[k, :, lanes] = (total * scale).astype(jnp.bfloat16)
                return carry

            lax.fori_loop(0, H, write, 0, unroll=4)
            pltpu.make_async_copy(rounded_ref.at[k], out_ref.at[k], sems.at[k]).start()
        for k in range(block):
            pltpu.make_async_copy(rounded_ref.at[k], out_ref.at[k], sems.at[k]).wait()


def stage(kind, peers, scalars, own, consts, halo=(), earlier=None, energy=None):
    totals = jax.ShapeDtypeStruct(own.shape, jnp.float32)
    operands = list(scalars) + [own] + list(consts) + list(halo)
    specs = [SMEM] * len(scalars) + [ANY] + [HBM] * 3 + [ANY] * len(halo)
    if earlier is not None:
        operands.append(earlier)
        specs.append(HBM if kind == "far" else ANY)
    if energy is not None:
        operands.append(energy)
        specs.append(VMEM)
    out_shapes, out_specs = [], []
    if kind != "rest":
        out_shapes.append(jax.ShapeDtypeStruct(own.shape, own.dtype) if kind == "far" else totals)
        out_specs.append(ANY if kind in ("own", "near") else HBM)
    if kind != "far":
        out_shapes.append(jax.ShapeDtypeStruct((peers if kind == "rest" else 8, L), jnp.float32))
        out_specs.append(VMEM)
    if kind == "own":
        out_shapes += [jax.ShapeDtypeStruct(own.shape[1:], own.dtype)] * 2
        out_specs += [HBM] * 2
    scratch = [
        pltpu.VMEM((8, L), jnp.float32),
        pltpu.VMEM(((H + 2 * PAD) * N + 2 * SHIFT, L), jnp.float32),
        pltpu.VMEM((ROWS, L), jnp.float32),
        pltpu.VMEM((ROWS, L), jnp.float32),
        pltpu.SemaphoreType.DMA((10,)),
        pltpu.VMEM(own.shape, own.dtype),
    ] + [pltpu.VMEM(c.shape, c.dtype) for c in consts]
    if halo:
        scratch.append(pltpu.VMEM((2, CHUNKS[kind][1]) + own.shape[1:], own.dtype))
    if kind != "rest":
        scratch.append(pltpu.VMEM(own.shape, jnp.float32))
    if kind == "far":
        scratch.append(pltpu.VMEM(own.shape, jnp.float32))
        scratch.append(pltpu.VMEM(own.shape, own.dtype))
    return pl.pallas_call(
        functools.partial(stage_kernel, kind),
        out_shape=out_shapes,
        in_specs=specs,
        out_specs=out_specs,
        scratch_shapes=scratch,
        compiler_params=pltpu.CompilerParams(vmem_limit_bytes=(56 if kind == "far" else 20) * 2**20),
        cost_estimate=pl.CostEstimate(flops=2 * 10**10, bytes_accessed=10**7, transcendentals=0),
    )(*operands)


def on_device(orbitals, exponents, offsets, pair_list):
    own = orbitals[0]
    block, _, width = own.shape
    groups = lax.axis_size("orb")
    peers = groups * lax.axis_size("spin")
    me = lax.axis_index("orb").astype(jnp.int32).reshape(1)
    up = [(k, (k + 1) % groups) for k in range(groups)]
    down = [(k, j) for j, k in up]
    consts = tuple(jnp.asarray(c) for c in tables())

    def exchange(array):
        return lax.ppermute(array, "orb", up), lax.ppermute(array, "orb", down)

    first, second = pair_list[0]
    live = first >= 0
    base = (me - 1) * block
    code = jnp.where(second < base, second + groups * block, second) - base
    code = jnp.where(code >= groups * block, code - groups * block, code)
    table = jnp.stack([jnp.where(live, first - me * block, -1), jnp.where(live, code, -1)])
    listing = jnp.pad(table.astype(own.dtype), ((0, LIST - 2), (0, width - table.shape[1])))
    sooner = CHUNKS["near"][1]
    near = exchange(jnp.concatenate([own[:sooner].reshape(sooner * N, width), listing], axis=0))
    rows = slice(sooner * N, sooner * N + 2)
    lists = [x[rows, : table.shape[1]].astype(jnp.int32) for x in near]
    around = jnp.concatenate([lists[0], table, lists[1]], axis=0)

    scalars = (me, offsets[0], exponents[0])
    acc, energy, second, last = stage("own", peers, scalars + (table,), own, consts)
    mid = exchange(second)
    far = exchange(last)
    scalars += (around,)
    acc, energy = stage("near", peers, scalars, own, consts, near, acc, energy)
    acc, energy = stage("mid", peers, scalars, own, consts, mid, acc, energy)
    (rows,) = stage("rest", peers, scalars, own, consts, far, energy=energy)
    rows = lax.all_to_all(rows, ("spin", "orb"), 0, 0)
    (potentials,) = stage("far", peers, scalars, own, consts, far, acc)
    return (potentials[None], jnp.sum(rows[:, 0]))


def solution(mesh):
    in_specs = (
        P("spin", "orb", None, None),
        P("spin", None),
        P("spin", None, None),
        P("spin", None, "orb"),
    )
    out_specs = (P("spin", "orb", None, None), P())
    return jax.shard_map(
        on_device, mesh=mesh, in_specs=in_specs, out_specs=out_specs, check_vma=False
    )
```
